128 devices in a mesh: dp: 64 (over z, y, x), tensor: 2 (over core).
Axes of the slice: x: 4, y: 4, z: 4, core: 2. Of those that a mesh axis runs over, the one named last changes fastest.
Arguments:
- tokens: bfloat16 [32768, 896], P(('dp', 'tensor')), may hold values from -12 to 12
- out_grad: bfloat16 [32768, 896], P(('dp', 'tensor')), may hold values from -24 to 24
- first_gain: float32 [896], replicated, may hold values from 0.25 to 1.75
- query_weight: bfloat16 [896, 896], P(None, 'tensor'), may hold values from -0.1875 to 0.1875
- query_bias: float32 [896], P('tensor'), may hold values from -3 to 3
- key_value_weight_pair: bfloat16 [2, 896, 128], P(None, None, 'tensor'), may hold values from -0.1875 to 0.1875
- key_value_bias_pair: float32 [2, 128], P(None, 'tensor'), may hold values from -3 to 3
- output_weight: bfloat16 [896, 896], P('tensor'), may hold values from -1.5 to 1.5
- second_gain: float32 [896], replicated, may hold values from 0.25 to 1.75
- gate_up_weight: bfloat16 [2, 896, 4864], P(None, None, 'tensor'), may hold values from -0.1875 to 0.1875
- down_weight: bfloat16 [4864, 896], P('tensor'), may hold values from -0.078125 to 0.078125
- lengths: int32 [256], replicated, may hold values from 0 to 512, as said below
- group_of: int32 [256], replicated, may hold values from 0 to 63, as said below
Outputs:
- result: bfloat16 [32768, 896], P(('dp', 'tensor'))
- grad_tokens: float32 [32768, 896], P(('dp', 'tensor'))
- grad_first_gain: float32 [896], replicated
- grad_query_weight: float32 [896, 896], P('dp', 'tensor')
- grad_query_bias: float32 [896], P('tensor')
- grad_key_value_weight: float32 [2, 896, 128], P(None, 'dp', 'tensor')
- grad_key_value_bias: float32 [2, 128], P(None, 'tensor')
- grad_output_weight: float32 [896, 896], P('tensor', 'dp')
- grad_second_gain: float32 [896], replicated
- grad_gate_up: float32 [2, 896, 4864], P(None, 'dp', 'tensor')
- grad_down: float32 [4864, 896], P('tensor', 'dp')
The draws below stay inside these ranges and needn't reach their ends.
Inputs may be any that keep to these rules, and one draw needn't show every extreme that they name: `lengths`: A length of 0 marks an unused sequence slot. The sequences of one data group hold at most 512 tokens together, exactly 512 in some group, and some sequence has 512 tokens. `group_of`: each data group receives 4 sequence slots.
All inputs are finite; a program needn't handle non-finite values.
Results may differ from the reference program's by a relative error of at most 0.014.
Values may be sent and summed in bfloat16 or wider, within the bound.
No kernel may reach another device: no remote copies, remote signals or barrier semaphores. Data moves between devices by JAX's collectives and lax.ppermute only.
A program may use at most 192 MiB of HBM per device.

```python
import math
import jax
import jax.numpy as jnp
from jax import lax

MODEL_WIDTH = 896
QUERY_HEADS = 14
KEY_VALUE_HEADS = 2
HEAD_SIZE = 64
FF = 4864
TOK_GRP = 512
SEQ_GRP = 4
SEQS = 256
TOKENS = 32768
N_DP = 64


def packing(key):
    blocks = SEQS // SEQ_GRP
    halfway = TOK_GRP // 2
    key_used, key_cuts, key_full, key_perm = jax.random.split(jax.random.fold_in(key, 101), 4)
    used = jax.random.randint(key_used, (blocks,), halfway + 1, TOK_GRP + 1)
    chosen = jax.random.randint(key_full, (), 0, blocks)
    block_ids = jnp.arange(blocks, dtype=jnp.int32)
    used = jnp.where(block_ids == chosen, TOK_GRP, used).astype(jnp.int32)
    cuts = jax.random.randint(key_cuts, (blocks, SEQ_GRP - 1), 0, used[:, None] + 1)
    cuts = cuts + (cuts == halfway).astype(jnp.int32)
    cuts = jnp.where(block_ids[:, None] == chosen, 0, cuts)
    cuts = jnp.sort(cuts, axis=1)
    edges = jnp.concatenate([jnp.zeros((blocks, 1), jnp.int32), cuts.astype(jnp.int32), used[:, None]], axis=1)
    lengths = (edges[:, 1:] - edges[:, :-1]).reshape(SEQS).astype(jnp.int32)
    order = jax.random.permutation(key_perm, blocks).astype(jnp.int32)
    group_of = jnp.repeat(order, SEQ_GRP).astype(jnp.int32)
    return (lengths, group_of)


def draw_lengths(key, part):
    lengths, group_of = packing(key)
    return lengths


def draw_group_of(key, part):
    lengths, group_of = packing(key)
    return group_of


def scaled_field(key, row_low, row_high, col_low, col_high):
    key_base, key_rows, key_cols = jax.random.split(key, 3)
    rows_scale = jnp.exp(jax.random.uniform(key_rows, (TOKENS, 1), minval=math.log(row_low), maxval=math.log(row_high)))
    cols_scale = jnp.exp(jax.random.uniform(key_cols, (1, MODEL_WIDTH), minval=math.log(col_low), maxval=math.log(col_high)))
    return (key_base, rows_scale, cols_scale)


def draw_tokens(key, part):
    key = jax.random.fold_in(key, 7)
    key_base, rows_scale, cols_scale = scaled_field(key, 0.3, 3.0, 0.4, 2.5)
    base = jax.random.normal(key_base, (TOKENS, MODEL_WIDTH))
    return jnp.clip(base * rows_scale * cols_scale, -12.0, 12.0).astype(jnp.bfloat16)


def spiked(result, rng, source, target, blocks, factor):
    owner, partner = [(jnp.arange(result.shape[dim]) // (result.shape[dim] // blocks)).reshape([-1 if axis == dim else 1 for axis in range(result.ndim)]) for dim in (source, target)]
    chosen = jax.random.permutation(rng, blocks)[partner]
    strong = (owner == chosen) | (owner == (partner + blocks // 2) % blocks)
    return jnp.where(strong, factor * result, result)


def levels(rng, shape, cuts, least, top_value):
    loudness = 1.0
    for dim, parts in cuts:
        steps = jax.random.uniform(jax.random.fold_in(jax.random.fold_in(rng, 6), dim), (parts,), jnp.float32, least / len(cuts), top_value / len(cuts))
        loudness = loudness * jnp.repeat(jnp.exp(steps), shape[dim] // parts).reshape((-1,) + (1,) * (len(shape) - 1 - dim))
    return loudness


def scatter_about(rng, extent, scale, limit, shards=(), kind=jnp.bfloat16):
    factor_of = levels(rng, extent, shards, -0.22, 0.18) if shards else 1.0
    result = jax.random.normal(rng, extent, jnp.float32) * scale * factor_of
    return jnp.minimum(jnp.maximum(result, -limit), limit).astype(kind)


def gaussian_with(key, shape, scale, bound, pieces, heavy, held_as=jnp.bfloat16):
    values = scale * jax.random.normal(key, shape, jnp.float32)
    if pieces:
        values = values * levels(key, shape, pieces, -0.22, 0.18)
    return jnp.clip(spiked(values, jax.random.fold_in(key, 3), *heavy), -bound, bound).astype(held_as)


def setup_inputs(seed: int = 0) -> dict:
    streams_of = jax.random.split(jax.random.key(seed), 14)
    return {
        "tokens": draw_tokens(jax.random.fold_in(streams_of[13], 71), 0),
        "out_grad": gaussian_with(streams_of[1], (TOKENS, MODEL_WIDTH), 1.0, 24.0, ((0, 128),), (0, 1, 128, 5.5)),
        "first_gain": jnp.clip(1.0 + 0.15 * jax.random.normal(streams_of[2], (MODEL_WIDTH,), jnp.float32), 0.25, 1.75),
        "query_weight": scatter_about(streams_of[3], (MODEL_WIDTH, QUERY_HEADS * HEAD_SIZE), MODEL_WIDTH ** -0.5, 0.1875, ((1, 2),)),
        "query_bias": scatter_about(streams_of[4], (QUERY_HEADS * HEAD_SIZE,), 0.5, 3.0, ((0, 2),), jnp.float32),
        "key_value_weight_pair": scatter_about(streams_of[5], (2, MODEL_WIDTH, KEY_VALUE_HEADS * HEAD_SIZE), MODEL_WIDTH ** -0.5, 0.1875, ((2, 2),)),
        "key_value_bias_pair": scatter_about(streams_of[6], (2, KEY_VALUE_HEADS * HEAD_SIZE), 0.5, 3.0, ((1, 2),), jnp.float32),
        "output_weight": scatter_about(streams_of[7], (QUERY_HEADS * HEAD_SIZE, MODEL_WIDTH), 16 ** -0.5, 1.5, ((0, 2),)),
        "second_gain": jnp.clip(1.0 + 0.15 * jax.random.normal(streams_of[8], (MODEL_WIDTH,), jnp.float32), 0.25, 1.75),
        "gate_up_weight": scatter_about(streams_of[9], (2, MODEL_WIDTH, FF), MODEL_WIDTH ** -0.5, 0.1875, ((2, 2),)),
        "down_weight": scatter_about(streams_of[10], (FF, MODEL_WIDTH), FF ** -0.5, 0.078125, ((0, 2),)),
        "lengths": draw_lengths(jax.random.fold_in(streams_of[13], 71), 0),
        "group_of": draw_group_of(jax.random.fold_in(streams_of[13], 71), 0),
    }


@jax.custom_vjp
def lower_half(v):
    return lax.optimization_barrier(v.astype(jnp.bfloat16)).astype(jnp.float32)

@jax.custom_vjp
def low_back(v):
    return v

def low_keep(v):
    return (lower_half(v), None)

def low_pass(kept, grad):
    return (grad,)

def back_keep(v):
    return (v, None)

def back_low(kept, grad):
    return (lower_half(grad),)
lower_half.defvjp(low_keep, low_pass)
low_back.defvjp(back_keep, back_low)
EPS = 1e-06
THETA = 1000000.0

def layout(lengths, group_of, data_group, slot_total_count):
    mine = jnp.where(group_of == data_group, lengths, 0).astype(jnp.int32)
    ends = jnp.cumsum(mine, dtype=jnp.int32)
    begins = ends - mine
    slots = jnp.arange(slot_total_count, dtype=jnp.int32)
    segment = lax.optimization_barrier(jnp.sum((ends[None, :] <= slots[:, None]).astype(jnp.int32), axis=1, dtype=jnp.int32))
    filled = jnp.sum(mine, dtype=jnp.int32)
    begin_all = jnp.concatenate([begins, filled[None]]).astype(jnp.int32)
    member = segment[:, None] == jnp.arange(lengths.shape[0] + 1, dtype=jnp.int32)[None, :]
    first_slot = lax.optimization_barrier(jnp.sum(jnp.where(member, begin_all[None, :], 0), axis=1, dtype=jnp.int32))
    return (segment, (slots - first_slot).astype(jnp.int32))

def rope_tables(position, size):
    halfway = size // 2
    freq = jnp.exp(jnp.arange(halfway, dtype=jnp.float32) * (-2.0 * math.log(THETA) / size))
    angle = position.astype(jnp.float32)[:, None] * freq[None, :]
    cosine_table = jnp.cos(angle)
    sine_table = jnp.sin(angle)
    return (jnp.concatenate([cosine_table, cosine_table], axis=1), jnp.concatenate([sine_table, sine_table], axis=1))

def rotary_embedding(value, cosine_table, sine_table):
    halfway = value.shape[-1] // 2
    turned = jnp.concatenate([-value[..., halfway:], value[..., :halfway]], axis=-1)
    return value * cosine_table[:, None, :] + turned * sine_table[:, None, :]

def matmul(left, right):
    return jnp.dot(left, right, precision=lax.Precision.HIGHEST)

def group_forward(params, group_tokens, segment, cosine_table, sine_table):
    first_gain, query_weight, query_bias, key_value_weight_pair, key_value_bias_pair, output_weight, second_gain, gate_up_weight, down_weight = params
    highest = lax.Precision.HIGHEST
    slot_total_count = group_tokens.shape[0]
    inv_first = lax.rsqrt(lax.optimization_barrier(jnp.mean(group_tokens * group_tokens, axis=1, keepdims=True)) + EPS)
    first = lower_half(group_tokens * inv_first * first_gain)
    query = low_back(matmul(first, query_weight) + query_bias)
    key_value_pair = low_back(jnp.einsum('td,sdc->stc', first, key_value_weight_pair, precision=highest) + key_value_bias_pair[:, None, :])
    rotated_query_rows = lower_half(rotary_embedding(query.reshape(slot_total_count, QUERY_HEADS, HEAD_SIZE), cosine_table, sine_table))
    rotated_key_rows = lower_half(rotary_embedding(key_value_pair[0].reshape(slot_total_count, KEY_VALUE_HEADS, HEAD_SIZE), cosine_table, sine_table))
    value_head_rows = lower_half(key_value_pair[1].reshape(slot_total_count, KEY_VALUE_HEADS, HEAD_SIZE))
    grouped_heads = rotated_query_rows.reshape(slot_total_count, KEY_VALUE_HEADS, QUERY_HEADS // KEY_VALUE_HEADS, HEAD_SIZE)
    scale = 1.0 / math.sqrt(HEAD_SIZE)
    scores = low_back(jnp.einsum('qkgd,skd->kgqs', grouped_heads, rotated_key_rows, precision=highest) * scale)
    slots = jnp.arange(slot_total_count, dtype=jnp.int32)
    allowed = (segment[:, None] == segment[None, :]) & (slots[None, :] <= slots[:, None])
    scores = jnp.where(allowed, scores, -1e+30)
    peak = lax.optimization_barrier(jnp.max(scores, axis=-1, keepdims=True))
    expo = jnp.exp(scores - peak)
    probs = expo / lax.optimization_barrier(jnp.sum(expo, axis=-1, keepdims=True))
    attended = low_back(jnp.einsum('kgqs,skd->qkgd', lower_half(probs), value_head_rows, precision=highest))
    attended = lower_half(attended.reshape(slot_total_count, QUERY_HEADS * HEAD_SIZE))
    branch = low_back(matmul(attended, output_weight))
    middle = group_tokens + branch
    inv_second = lax.rsqrt(lax.optimization_barrier(jnp.mean(middle * middle, axis=1, keepdims=True)) + EPS)
    second = lower_half(middle * inv_second * second_gain)
    gate_up = low_back(jnp.einsum('td,sdf->stf', second, gate_up_weight, precision=highest))
    hidden = lower_half(jax.nn.silu(gate_up[0]) * gate_up[1])
    return middle + matmul(hidden, down_weight)

def reference(tokens, out_grad, first_gain, query_weight, query_bias, key_value_weight_pair, key_value_bias_pair, output_weight, second_gain, gate_up_weight, down_weight, lengths, group_of):
    params = (first_gain.astype(jnp.float32), query_weight.astype(jnp.float32), query_bias.astype(jnp.float32), key_value_weight_pair.astype(jnp.float32), key_value_bias_pair.astype(jnp.float32), output_weight.astype(jnp.float32), second_gain.astype(jnp.float32), gate_up_weight.astype(jnp.float32), down_weight.astype(jnp.float32))
    token_groups = tokens.astype(jnp.float32).reshape(N_DP, TOK_GRP, MODEL_WIDTH)
    grad_groups = out_grad.astype(jnp.float32).reshape(N_DP, TOK_GRP, MODEL_WIDTH)
    zeros = jax.tree.map(jnp.zeros_like, params)

    def step(totals, item):
        data_group, group_tokens, group_grad = item
        segment, position = layout(lengths, group_of, data_group, TOK_GRP)
        cosine_table, sine_table = rope_tables(position, HEAD_SIZE)
        outputs, pull = jax.vjp(lambda weights, inputs: group_forward(weights, inputs, segment, cosine_table, sine_table), params, group_tokens)
        weight_grads, token_grads = pull(group_grad)
        totals = jax.tree.map(lambda left, right: left + right, totals, weight_grads)
        return (totals, (outputs, token_grads))
    totals, (outputs, token_grads) = lax.scan(step, zeros, (jnp.arange(N_DP, dtype=jnp.int32), token_groups, grad_groups))
    return (outputs.reshape(TOKENS, MODEL_WIDTH).astype(jnp.bfloat16), token_grads.reshape(TOKENS, MODEL_WIDTH), totals[0], totals[1], totals[2], totals[3], totals[4], totals[5], totals[6], totals[7], totals[8])
```

```python
import math

import jax
import jax.numpy as jnp
import numpy as np
from jax import lax
from jax.sharding import Mesh
from jax.sharding import PartitionSpec as P

HEAD_SIZE = 64
DP = ("dp_0", "dp_1", "dp_2")
DP_TENSOR = ("dp_0", "dp_1", "dp_2", "tensor")
EPS = 1e-06
THETA = 1000000.0
BF16 = jnp.bfloat16
F32 = jnp.float32
RING = 4
GATE, UP, NATURAL = (1, 2, 0), (2, 1, 0), (0, 1, 2)
STRIDES = (16, 4, 1)


def dot(left, right):
    return jnp.dot(left, right, preferred_element_type=F32)


def contract(left, right, left_dim, right_dim):
    return lax.dot_general(
        left, right, (((left_dim,), (right_dim,)), ((), ())), preferred_element_type=F32
    )


def swap(x):
    return lax.ppermute(x, "tensor", [(0, 1), (1, 0)])


def swap_rows(x):
    half = x.shape[0] // 2
    other = swap(x)
    return jnp.concatenate([other[half:], other[:half]], axis=0)


def shift(x, axis, by):
    return lax.ppermute(x, axis, [(i, (i + by) % RING) for i in range(RING)])


def ring_order(size):
    a, b = range(size // 2), range(size // 2, size)
    runs = ((2, a), (1, b), (2, b), (3, a), (1, a), (3, b), (0, a), (0, b))
    return [(off, row) for off, rows in runs for row in rows]


def direct_order(size):
    return [(off, row) for off in (1, 3, 2, 0) for row in range(size)]


def row_offsets(rows_per_device, first_order):
    q = rows_per_device
    second = [(off, *direct_order(q)[row]) for off, row in direct_order(RING * q)]
    return np.array(
        [(off, *second[row]) for off, row in first_order(RING * RING * q)], np.int32
    )


def permuted(x, order, rows_per_device, first_order):
    table = row_offsets(rows_per_device, first_order)
    index = jnp.asarray(table[:, 3])
    for stage, axis in enumerate(order):
        coordinate = (lax.axis_index(DP[axis]) + jnp.asarray(table[:, stage])) % RING
        index = index + rows_per_device * STRIDES[axis] * coordinate
    width = x.shape[1]
    hot = (index[:, None] == jnp.arange(width, dtype=jnp.int32)[None, :]).astype(BF16)
    return contract(hot, x, 1, 1).astype(BF16)


def ring_first(send_right, send_left, axis):
    return shift(send_right, axis, 1), shift(send_left, axis, 3)


def ring_second(from_left, from_right, later, axis):
    h = later.shape[0] // 2
    right = (later[:h].astype(F32) + from_left[:h].astype(F32)).astype(BF16)
    left = (later[h:].astype(F32) + from_right[:h].astype(F32)).astype(BF16)
    return shift(right, axis, 1), shift(left, axis, 3)


def ring_sum(from_left, from_right, last_left, last_right, own):
    h = own.shape[0] // 2
    head = own[:h].astype(F32) + from_right[h:].astype(F32) + last_left.astype(F32)
    tail = own[h:].astype(F32) + from_left[h:].astype(F32) + last_right.astype(F32)
    return jnp.concatenate([head, tail], axis=0)


def direct_sends(block, axis):
    q = block.shape[0] // RING
    low = block.astype(BF16)
    return [shift(low[k * q : (k + 1) * q], axis, by) for k, by in enumerate((1, 3, 2))]


def direct_sum(block, arrived):
    q = block.shape[0] // RING
    out = block[3 * q :].astype(F32)
    for piece in arrived:
        out = out + piece.astype(F32)
    return out


def row_blocks(left_t, right, which):
    q = left_t.shape[0] // RING
    return [dot(left_t[k * q : (k + 1) * q], right).astype(BF16) for k in which]


def scatter_natural(x, axis):
    x = x.reshape(RING, x.shape[0] // RING, x.shape[1])
    return lax.psum_scatter(x, axis, scatter_dimension=0, tiled=True)[0]


def direct_stage_with_sums(block, sums, axis):
    q, n = block.shape[0] // RING, block.shape[1]
    extra = -(-2 * sums.shape[0] // n)
    extra = -(-extra // 16) * 16
    high = sums.astype(BF16)
    low = (sums - high.astype(F32)).astype(BF16)
    sums = high.astype(F32) + low.astype(F32)
    packed = jnp.concatenate(
        [high, low, jnp.zeros((extra * n - 2 * sums.shape[0],), BF16)]
    ).reshape(extra, n)
    rounded = block.astype(BF16)
    out = block[3 * q :].astype(F32)
    heard = []
    arrived = [
        shift(jnp.concatenate([packed, rounded[k * q : (k + 1) * q]], axis=0), axis, by)
        for k, by in enumerate((1, 3, 2))
    ]
    m = sums.shape[0]
    for piece in arrived:
        out = out + piece[extra:].astype(F32)
        flat = piece[:extra].reshape(extra * n).astype(F32)
        heard.append(flat[:m] + flat[m : 2 * m])
    return out, (sums + heard[2]) + (heard[0] + heard[1])


def pinned(*xs):
    return lax.optimization_barrier(xs)


def layout(lengths, group_of, data_group, slots):
    mine = jnp.where(group_of == data_group, lengths, 0)
    ends = jnp.cumsum(mine, dtype=jnp.int32)
    past = ends[None, :] <= slots[:, None]
    segment = jnp.sum(past.astype(jnp.int32), axis=1, dtype=jnp.int32)
    first_slot = jnp.sum(jnp.where(past, mine[None, :], 0), axis=1, dtype=jnp.int32)
    return (segment, slots - first_slot)


def rope_tables(position, size):
    halfway = size // 2
    freq = jnp.exp(jnp.arange(halfway, dtype=F32) * (-2.0 * math.log(THETA) / size))
    angle = position.astype(F32)[:, None] * freq[None, :]
    cosine = jnp.cos(angle)
    sine = jnp.sin(angle)
    return (
        jnp.concatenate([cosine, cosine], axis=1),
        jnp.concatenate([sine, sine], axis=1),
    )


def rotary(value, cosine, sine):
    halfway = value.shape[-1] // 2
    turned = jnp.concatenate([-value[..., halfway:], value[..., :halfway]], axis=-1)
    return value * cosine[:, None, :] + turned * sine[:, None, :]


def rope_back(grad, cosine, sine):
    halfway = grad.shape[-1] // 2
    scaled = grad * sine[:, None, :]
    return grad * cosine[:, None, :] + jnp.concatenate(
        [scaled[..., halfway:], -scaled[..., :halfway]], axis=-1
    )


def body(
    tokens,
    out_grad,
    first_gain,
    query_weight,
    query_bias,
    key_value_weight_pair,
    key_value_bias_pair,
    output_weight,
    second_gain,
    gate_up_weight,
    down_weight,
    lengths,
    group_of,
):
    own_rows, width = tokens.shape
    rows = 2 * own_rows
    tensor_rank = lax.axis_index("tensor")
    data_group = lax.axis_index(DP)
    heads = query_weight.shape[1] // HEAD_SIZE
    scale = 1.0 / math.sqrt(HEAD_SIZE)
    per_device = width // 64
    slots = (jnp.arange(rows, dtype=jnp.int32) + tensor_rank * own_rows) % rows
    segment, position = layout(lengths, group_of, data_group, slots)
    cosine, sine = rope_tables(position, HEAD_SIZE)
    allowed = (segment[:, None] == segment[None, :]) & (slots[None, :] <= slots[:, None])

    tokens_all = jnp.concatenate([tokens, swap(tokens)], axis=0)
    grad_all = jnp.concatenate([out_grad, swap(out_grad)], axis=0)
    inputs = tokens_all.astype(F32)
    inv_first = lax.rsqrt(jnp.mean(inputs * inputs, axis=1, keepdims=True) + EPS)
    normed_first = inputs * inv_first
    first = (normed_first * first_gain).astype(BF16)
    query = dot(first, query_weight) + query_bias
    keys = dot(first, key_value_weight_pair[0]) + key_value_bias_pair[0]
    values = dot(first, key_value_weight_pair[1]) + key_value_bias_pair[1]
    rq = rotary(query.reshape(rows, heads, HEAD_SIZE), cosine, sine).astype(BF16)
    rk = rotary(keys[:, None, :], cosine, sine)[:, 0].astype(BF16)
    vals = values.astype(BF16)

    scores = jnp.einsum("qgd,sd->gqs", rq, rk, preferred_element_type=F32) * scale
    scores = jnp.where(allowed[None], scores, -1e30)
    peak = jnp.max(scores, axis=-1, keepdims=True)
    expo = jnp.exp(scores - peak)
    probs = expo / jnp.sum(expo, axis=-1, keepdims=True)
    probs_low = probs.astype(BF16)
    attended = jnp.einsum("gqs,sd->qgd", probs_low, vals, preferred_element_type=F32)
    attended = attended.reshape(rows, heads * HEAD_SIZE).astype(BF16)
    branch = dot(attended, output_weight).astype(BF16)
    middle = inputs + (branch.astype(F32) + swap_rows(branch).astype(F32))
    inv_second = lax.rsqrt(jnp.mean(middle * middle, axis=1, keepdims=True) + EPS)
    normed_second = middle * inv_second
    second = (normed_second * second_gain).astype(BF16)

    gate = dot(second, gate_up_weight[0])
    up = dot(second, gate_up_weight[1])
    sigmoid = jax.nn.sigmoid(gate)
    activated = gate * sigmoid
    hidden = (activated * up).astype(BF16)
    grad_down_part = contract(grad_all, hidden, 0, 0).astype(BF16)
    grad_late, grad_down_part = pinned(grad_all, grad_down_part)
    down_first = scatter_natural(grad_down_part, DP[0])
    d_hidden = contract(grad_late, down_weight, 1, 1)
    d_gate = (d_hidden * up * sigmoid * (1.0 + gate * (1.0 - sigmoid))).astype(BF16)
    d_up = (d_hidden * activated).astype(BF16)
    gate_left = permuted(second, GATE, per_device, ring_order)
    up_left = permuted(second, UP, per_device, ring_order)
    gate_axes = [DP[axis] for axis in GATE]
    up_axes = [DP[axis] for axis in UP]
    gate_sent = row_blocks(gate_left, d_gate, (0, 1))
    up_sent = row_blocks(up_left, d_up, (0, 1))
    gate_first = ring_first(*gate_sent, gate_axes[0])
    up_first = ring_first(*up_sent, up_axes[0])
    gate_kept = row_blocks(gate_left, d_gate, (2, 3))
    up_kept = row_blocks(up_left, d_up, (2, 3))

    d_gate, d_up, gate_sent, up_sent = pinned(d_gate, d_up, gate_sent, up_sent)
    d_second_part = contract(d_gate, gate_up_weight[0], 1, 1) + contract(
        d_up, gate_up_weight[1], 1, 1
    )
    second_gain_part = jnp.sum(d_second_part * normed_second, axis=0)
    d_second_low = d_second_part.astype(BF16)
    d_second = d_second_low.astype(F32) + swap_rows(d_second_low).astype(F32)
    mlp = dot(hidden, down_weight)
    mlp_own = mlp[:own_rows] + swap(mlp[own_rows:].astype(BF16)).astype(F32)
    result = (middle[:own_rows] + mlp_own).astype(BF16)
    d_normed = d_second * second_gain
    d_middle = grad_all.astype(F32) + inv_second * (
        d_normed - normed_second * jnp.mean(d_normed * normed_second, axis=1, keepdims=True)
    )
    d_branch = d_middle.astype(BF16)
    output_block = dot(permuted(d_branch, NATURAL, per_device, direct_order), attended)
    output_block = output_block.astype(BF16)
    output_arrived = direct_sends(output_block, DP[0])

    d_attended = contract(d_branch, output_weight, 1, 1).astype(BF16)
    d_attended = d_attended.reshape(rows, heads, HEAD_SIZE)
    d_probs = jnp.einsum("qgd,sd->gqs", d_attended, vals, preferred_element_type=F32)
    inner = jnp.sum(probs * d_probs, axis=-1, keepdims=True)
    d_scores = (probs * (d_probs - inner)).astype(BF16)
    d_scores, gate_first, up_first, down_first = pinned(
        d_scores, gate_first, up_first, down_first
    )
    down_second = scatter_natural(down_first, DP[1])
    gate_second = ring_second(*gate_first, gate_kept[0], gate_axes[0])
    up_second = ring_second(*up_first, up_kept[0], up_axes[0])

    d_rq = jnp.einsum("gqs,sd->qgd", d_scores, rk, preferred_element_type=F32) * scale
    d_rk = jnp.einsum("gqs,qgd->sd", d_scores, rq, preferred_element_type=F32) * scale
    d_values = jnp.einsum("gqs,qgd->sd", probs_low, d_attended, preferred_element_type=F32)
    d_query = rope_back(d_rq, cosine, sine).reshape(rows, heads * HEAD_SIZE).astype(BF16)
    d_keys = rope_back(d_rk[:, None, :], cosine, sine)[:, 0].astype(BF16)
    d_values = d_values.astype(BF16)
    d_all = jnp.concatenate([d_query, d_keys, d_values], axis=1)
    d_all, gate_second, up_second, output_arrived = pinned(
        d_all, gate_second, up_second, output_arrived
    )
    gate_block = ring_sum(*gate_first, *gate_second, gate_kept[1])
    up_block = ring_sum(*up_first, *up_second, up_kept[1])
    gate_arrived = direct_sends(gate_block, gate_axes[1])
    up_arrived = direct_sends(up_block, up_axes[1])
    output_block = direct_sum(output_block, output_arrived)
    first_left = permuted(first, NATURAL, per_device, direct_order)
    pair_product = dot(first_left, d_all)
    d_first_part = (
        contract(d_query, query_weight, 1, 1)
        + contract(d_keys, key_value_weight_pair[0], 1, 1)
        + contract(d_values, key_value_weight_pair[1], 1, 1)
    )
    first_gain_part = jnp.sum(d_first_part * normed_first, axis=0)
    d_first = d_first_part[:own_rows] + swap(d_first_part[own_rows:].astype(BF16)).astype(F32)
    gains = jnp.concatenate([first_gain_part, second_gain_part])
    gains = gains + swap(gains)
    sums = jnp.concatenate([gains, jnp.sum(d_all.astype(F32), axis=0)])
    block, sums = direct_stage_with_sums(pair_product, sums, DP[0])

    block, gate_arrived, up_arrived, down_second = pinned(
        block, gate_arrived, up_arrived, down_second
    )
    grad_down = scatter_natural(down_second, DP[2])
    block = jnp.concatenate([block, output_block], axis=1)
    block, sums = direct_stage_with_sums(block, sums, DP[1])
    both = jnp.concatenate(
        [direct_sum(gate_block, gate_arrived), direct_sum(up_block, up_arrived)], axis=1
    )
    both = direct_sum(both, direct_sends(both, DP[0]))
    block, sums = direct_stage_with_sums(block, sums, DP[2])

    d_normed = d_first * first_gain
    own_normed = normed_first[:own_rows]
    grad_tokens = d_middle[:own_rows] + inv_first[:own_rows] * (
        d_normed - own_normed * jnp.mean(d_normed * own_normed, axis=1, keepdims=True)
    )
    n = heads * HEAD_SIZE
    ff = d_gate.shape[1]
    biases = sums[2 * width :]
    return (
        result,
        grad_tokens,
        sums[:width],
        block[:, :n],
        biases[:n],
        jnp.stack([block[:, n : n + HEAD_SIZE], block[:, n + HEAD_SIZE : n + 2 * HEAD_SIZE]]),
        biases[n:].reshape(2, HEAD_SIZE),
        block[:, n + 2 * HEAD_SIZE :].T,
        sums[width : 2 * width],
        jnp.stack([both[:, :ff], both[:, ff:]]),
        grad_down.astype(F32).T,
    )


def solution(mesh):
    torus = Mesh(
        mesh.devices.reshape(4, 4, 4, mesh.shape["tensor"]), ("dp_0", "dp_1", "dp_2", "tensor")
    )
    placed = (
        P(DP_TENSOR, None),
        P(DP_TENSOR, None),
        P(),
        P(None, "tensor"),
        P("tensor"),
        P(None, None, "tensor"),
        P(None, "tensor"),
        P("tensor", None),
        P(),
        P(None, None, "tensor"),
        P("tensor", None),
        P(),
        P(),
    )
    return jax.shard_map(
        body,
        mesh=torus,
        in_specs=placed,
        out_specs=(
            P(DP_TENSOR, None),
            P(DP_TENSOR, None),
            P(),
            P(DP, "tensor"),
            P("tensor"),
            P(None, DP, "tensor"),
            P(None, "tensor"),
            P("tensor", DP),
            P(),
            P(None, DP, "tensor"),
            P("tensor", DP),
        ),
        check_vma=False,
    )
```

```python
import math

import jax
import jax.numpy as jnp
import numpy as np
from jax import lax
from jax.experimental import pallas as pl
from jax.experimental.pallas import tpu as pltpu
from jax.sharding import Mesh
from jax.sharding import PartitionSpec as P

HEAD_SIZE = 64
DP = ("dp_0", "dp_1", "dp_2")
DP_TENSOR = ("dp_0", "dp_1", "dp_2", "tensor")
EPS = 1e-06
THETA = 1000000.0
BF16 = jnp.bfloat16
F32 = jnp.float32
RING = 4
GATE = ((1, True), (2, False), (0, False))
UP = ((2, True), (1, False), (0, False))
PAIR = ((1, False), (2, False), (0, False))
BRANCH = ((2, False), (1, False), (0, False))
ORDERS = (GATE, UP, PAIR, BRANCH)
SUM_ROWS, SUM_LANES = 8, 512
STRIDES = (16, 4, 1)


def dot(left, right):
    return jnp.dot(left, right, preferred_element_type=F32)


def contract(left, right, left_dim, right_dim):
    return lax.dot_general(
        left, right, (((left_dim,), (right_dim,)), ((), ())), preferred_element_type=F32
    )


def swap(x):
    return lax.ppermute(x, "tensor", [(0, 1), (1, 0)])


def swap_rows(x):
    half = x.shape[0] // 2
    other = swap(x)
    return jnp.concatenate([other[half:], other[:half]], axis=0)


def shift(x, axis, by):
    return lax.ppermute(x, axis, [(i, (i + by) % RING) for i in range(RING)])


def stage_order(ring, size):
    if ring:
        a, b = range(size // 2), range(size // 2, size)
        runs = ((2, a), (1, b), (2, b), (3, a), (1, a), (3, b), (0, a), (0, b))
        return [(off, row) for off, rows in runs for row in rows]
    return [(off, row) for off in (1, 3, 2, 0) for row in range(size)]


def offset_columns(order, rows_per_device):
    table = [(row,) for row in range(rows_per_device)]
    for _, ring in reversed(order):
        table = [(off, *table[row]) for off, row in stage_order(ring, len(table))]
    table = np.array(table, np.int32)
    stages = [axis for axis, _ in order]
    return [table[:, stages.index(axis)] for axis in range(3)] + [table[:, 3]]


def offset_table(rows_per_device):
    columns = [c for order in ORDERS for c in offset_columns(order, rows_per_device)]
    return np.stack(columns, axis=1)


def ring_first(send_right, send_left, axis):
    return shift(send_right, axis, 1), shift(send_left, axis, 3)


def to_others(pieces, axis):
    return [shift(piece, axis, by) for piece, by in zip(pieces, (1, 3, 2))]


def scatter_natural(x, axis):
    x = x.reshape(RING, x.shape[0] // RING, x.shape[1])
    return lax.psum_scatter(x, axis, scatter_dimension=0, tiled=True)[0]


def pinned(*xs):
    return lax.optimization_barrier(xs)


def layout(lengths, group_of, data_group, slots):
    mine = jnp.where(group_of == data_group, lengths, 0)
    ends = jnp.cumsum(mine, dtype=jnp.int32)
    past = ends[None, :] <= slots[:, None]
    return jnp.sum(jnp.where(past, mine[None, :], 0), axis=1, dtype=jnp.int32)


def rope_table(position):
    halfway = HEAD_SIZE // 2
    lane = np.arange(4 * halfway)
    freq = np.exp((lane % halfway) * (-2.0 * math.log(THETA) / HEAD_SIZE)).astype(np.float32)
    phase = np.where(lane < HEAD_SIZE, math.pi / 2, 0.0).astype(np.float32)
    return jnp.sin(position.astype(F32)[:, None] * freq[None, :] + phase)


def wide_tables(table):
    low = iota(table.shape, 1) < HEAD_SIZE
    other = rolled(table)
    return jnp.where(low, table, other), jnp.where(low, other, -table)


VMEM_LIMIT = 60 * 1024 * 1024
WIDE = 2 * HEAD_SIZE


def nt(left, right):
    return contract(left, right, 1, 1)


def tn(left, right):
    return contract(left, right, 0, 0)


def whole(*shape):
    return pl.BlockSpec(shape, lambda *_: (0,) * len(shape))


def iota(shape, dim):
    return lax.broadcasted_iota(jnp.int32, shape, dim)


def sent_rows(here_ref, table_ref, which):
    base = 4 * which
    rows = table_ref[:, base + 3 : base + 4]
    count = table_ref.shape[0] // 64
    for k, stride in enumerate(STRIDES):
        at = (table_ref[:, base + k : base + k + 1] + here_ref[1 + k]) & (RING - 1)
        rows = rows + count * stride * at
    return rows


def permuted_rows(index, x):
    width = x.shape[1]
    hot = jnp.where(index == iota((width, width), 1), 1.0, 0.0).astype(BF16)
    return nt(hot, x).astype(BF16)


def widen(heads):
    shape = (heads * WIDE, heads * HEAD_SIZE)
    row, col = iota(shape, 1), iota(shape, 0)
    inner = col % WIDE
    here = (col // WIDE) * HEAD_SIZE + inner
    half = HEAD_SIZE // 2
    e = inner - HEAD_SIZE
    turned = (col // WIDE) * HEAD_SIZE + jnp.where(e < half, e + half, e - half)
    sign = jnp.where(inner < HEAD_SIZE, 1.0, jnp.where(e < half, -1.0, 1.0))
    source = jnp.where(inner < HEAD_SIZE, here, turned)
    return jnp.where(row == source, sign, 0.0)


def rolled(x):
    return pltpu.roll(x, HEAD_SIZE, 1)


def slot_of(row, rank, rows):
    slot = row + rank * (rows // 2)
    return jnp.where(slot >= rows, slot - rows, slot)


def allowed_keys(first_slot, start, rank, rows):
    n = first_slot.shape[0]
    key = slot_of(iota((n, rows), 1), rank, rows)
    query = slot_of(iota((n, 1), 0) + start, rank, rows)
    return (key <= query) & (key >= first_slot)


def attend_kernel(
    here_ref, own_ref, other_ref, gain_ref, wq_ref, bq_ref, wkv_ref, bkv_ref, wo_ref, place_ref,
    rope_ref, table_ref,
    first_t_ref, q_ref, k_ref, v_ref, att_ref, stat_ref, branch_ref, first_ref,
):
    rows = q_ref.shape[0]
    half = rows // 2
    heads = wq_ref.shape[0] // HEAD_SIZE
    scale = 0.5 / math.sqrt(HEAD_SIZE)
    highest = lax.Precision.HIGHEST
    wide = widen(heads)
    both_last = (((1,), (1,)), ((), ()))
    wq = dot(wide.astype(BF16), wq_ref[...]).astype(BF16)
    bq = lax.dot_general(
        bq_ref[...], wide, both_last, precision=highest, preferred_element_type=F32
    )
    wide_one = widen(1)
    wk = dot(wide_one.astype(BF16), wkv_ref[0]).astype(BF16)
    bk = lax.dot_general(
        bkv_ref[0:1], wide_one, both_last, precision=highest, preferred_element_type=F32
    )
    for r, src in enumerate((own_ref, other_ref)):
        part = pl.ds(r * half, half)
        x = src[...].astype(F32)
        inv = lax.rsqrt(jnp.mean(x * x, axis=1, keepdims=True) + EPS)
        first = (x * inv * gain_ref[...]).astype(BF16)
        first_ref[part, :] = first
        cosine, sine = wide_tables(rope_ref[part, :])
        q = nt(first, wq) + bq
        for h in range(heads):
            qh = q[:, h * WIDE : (h + 1) * WIDE]
            q_ref[part, h * WIDE : (h + 1) * WIDE] = (qh * cosine + rolled(qh) * sine).astype(BF16)
        k = nt(first, wk) + bk
        k_ref[part, :] = (k * cosine + rolled(k) * sine).astype(BF16)
        v = (nt(first, wkv_ref[1]) + bkv_ref[1:2]).astype(BF16)
        v_ref[part, :] = jnp.concatenate([v, jnp.zeros_like(v)], axis=1)
    first_t_ref[...] = permuted_rows(sent_rows(here_ref, table_ref, 2), first_ref[...])
    keys, v_even = k_ref[...], v_ref[...]
    v_odd = rolled(v_even.astype(F32)).astype(BF16)
    rank = here_ref[0]
    for r in range(2):
        part = pl.ds(r * half, half)
        ok = allowed_keys(place_ref[part, :], r * half, rank, rows)
        stat = jnp.zeros((half, WIDE), F32)
        lane = iota((half, WIDE), 1)
        pair = None
        for h in range(heads):
            s = nt(q_ref[part, h * WIDE : (h + 1) * WIDE], keys) * scale
            s = jnp.where(ok, s, -1e30)
            peak = jnp.max(s, axis=1, keepdims=True)
            e = jnp.exp(s - peak)
            total = jnp.sum(e, axis=1, keepdims=True)
            p = (e * (1.0 / total)).astype(BF16)
            stat = jnp.where(lane == h, peak + jnp.log(total), stat)
            a = dot(p, v_odd if h % 2 else v_even)
            if h % 2:
                att_ref[part, (h // 2) * WIDE : (h // 2 + 1) * WIDE] = (pair + a).astype(BF16)
            else:
                pair = a
        if heads % 2:
            att_ref[part, (heads - 1) * HEAD_SIZE :] = pair[:, :HEAD_SIZE].astype(BF16)
        stat_ref[part, :] = stat
        branch_ref[part, :] = dot(att_ref[part, :], wo_ref[...]).astype(BF16)


def attend(here, own, other, gain, wq, bq, wkv, bkv, wo, place, rope, table):
    rows, width = 2 * own.shape[0], own.shape[1]
    heads = wq.shape[0] // HEAD_SIZE
    sds = jax.ShapeDtypeStruct
    outs = (
        sds((width, rows), BF16),
        sds((rows, heads * WIDE), BF16),
        sds((rows, WIDE), BF16),
        sds((rows, WIDE), BF16),
        sds((rows, heads * HEAD_SIZE), BF16),
        sds((rows, WIDE), F32),
        sds((rows, width), BF16),
    )
    return pl.pallas_call(
        attend_kernel,
        out_shape=outs,
        in_specs=[pl.BlockSpec(memory_space=pltpu.SMEM)]
        + [pl.BlockSpec(memory_space=pltpu.VMEM)] * 11,
        out_specs=[pl.BlockSpec(memory_space=pltpu.VMEM)] * 7,
        scratch_shapes=[pltpu.VMEM((rows, width), BF16)],
        compiler_params=pltpu.CompilerParams(vmem_limit_bytes=VMEM_LIMIT),
        cost_estimate=pl.CostEstimate(flops=5_000_000_000, bytes_accessed=8_000_000, transcendentals=0),
        name="attention_forward",
    )(here, own, other, gain, wq, bq, wkv, bkv, wo, place, rope, table)


def feed_forward_kernel(
    own_ref, other_ref, branch_ref, far_ref, gain_ref, og_own_ref, og_other_ref, wgu_ref, wd_ref,
    down_ref, dg_ref, du_ref, mid_ref, second_ref, res_ref, send_ref, ds_ref, gainsum_ref,
    og_ref, ot_ref, mlp_ref, acc_ref,
):
    step = pl.program_id(0)
    last = pl.num_programs(0) - 1
    half, width = own_ref.shape

    @pl.when(step == 0)
    def _():
        for r, tok in enumerate((own_ref, other_ref)):
            a, b = pl.ds(r * half, half), pl.ds((1 - r) * half, half)
            mid = tok[...].astype(F32) + (
                branch_ref[a, :].astype(F32) + far_ref[b, :].astype(F32)
            )
            mid_ref[a, :] = mid
            inv = lax.rsqrt(jnp.mean(mid * mid, axis=1, keepdims=True) + EPS)
            second_ref[a, :] = (mid * inv * gain_ref[...]).astype(BF16)
        for r, og in enumerate((og_own_ref, og_other_ref)):
            og_ref[r * half : (r + 1) * half, :] = og[...]
            ot_ref[:, r * half : (r + 1) * half] = og[...].T
        mlp_ref[...] = jnp.zeros_like(mlp_ref)
        acc_ref[...] = jnp.zeros_like(acc_ref)

    def units(n):
        wg, wu, wd = wgu_ref[0, :, :n], wgu_ref[1, :, :n], wd_ref[:n, :]
        second = second_ref[...]
        gate, up = dot(second, wg), dot(second, wu)
        d_hidden = nt(og_ref[...], wd)
        sigmoid = 1.0 / (1.0 + jnp.exp(-gate))
        act = gate * sigmoid
        hidden = (act * up).astype(BF16)
        d_gate = (d_hidden * up * (sigmoid * (1.0 + gate * (1.0 - sigmoid)))).astype(BF16)
        d_up = (d_hidden * act).astype(BF16)
        dg_ref[:, :n] = d_gate
        du_ref[:, :n] = d_up
        down_ref[:, :n] = dot(ot_ref[...], hidden).astype(BF16)
        mlp_ref[...] += dot(hidden, wd)
        acc_ref[...] += nt(d_gate, wg) + nt(d_up, wu)

    full = wd_ref.shape[0]
    tail = FF_LOCAL % full

    @pl.when(step < last)
    def _():
        units(full)

    @pl.when(step == last)
    def _():
        units(tail or full)
        res_ref[...] = mid_ref[:half, :] + mlp_ref[:half, :]
        send_ref[...] = mlp_ref[half:, :].astype(BF16)
        ds = acc_ref[...]
        ds_ref[...] = ds.astype(BF16)
        mid = mid_ref[...]
        normed = mid * lax.rsqrt(jnp.mean(mid * mid, axis=1, keepdims=True) + EPS)
        gainsum_ref[...] = jnp.sum(ds * normed, axis=0, keepdims=True)


def unit_products_kernel(
    here_ref, second_ref, table_ref, dg_ref, du_ref,
    g0_ref, g1_ref, g2_ref, g3_ref, u0_ref, u1_ref, u2_ref, u3_ref,
    gt_ref, ut_ref,
):
    quarter = g0_ref.shape[0]

    @pl.when(pl.program_id(0) == 0)
    def _():
        gt_ref[...] = permuted_rows(sent_rows(here_ref, table_ref, 0), second_ref[...])
        ut_ref[...] = permuted_rows(sent_rows(here_ref, table_ref, 1), second_ref[...])

    for k, ref in enumerate((g0_ref, g1_ref, g2_ref, g3_ref)):
        ref[...] = dot(gt_ref[k * quarter : (k + 1) * quarter, :], dg_ref[...]).astype(BF16)
    for k, ref in enumerate((u0_ref, u1_ref, u2_ref, u3_ref)):
        ref[...] = dot(ut_ref[k * quarter : (k + 1) * quarter, :], du_ref[...]).astype(BF16)


FF_LOCAL = 2432
FF_BLOCK = 512


def feed_forward(own, other, branch, far, gain, og_own, og_other, wgu, wd):
    half, width = own.shape
    rows = 2 * half
    ff = wd.shape[0]
    sds = jax.ShapeDtypeStruct
    units = pl.BlockSpec((rows, FF_BLOCK), lambda i: (0, i))
    return pl.pallas_call(
        feed_forward_kernel,
        grid=(-(-ff // FF_BLOCK),),
        out_shape=[
            sds((width, ff), BF16),
            sds((rows, ff), BF16),
            sds((rows, ff), BF16),
            sds((rows, width), F32),
            sds((rows, width), BF16),
            sds((half, width), F32),
            sds((half, width), BF16),
            sds((rows, width), BF16),
            sds((1, width), F32),
        ],
        in_specs=[
            whole(half, width), whole(half, width), whole(rows, width), whole(rows, width),
            whole(1, width), whole(half, width), whole(half, width),
            pl.BlockSpec((2, width, FF_BLOCK), lambda i: (0, 0, i)),
            pl.BlockSpec((FF_BLOCK, width), lambda i: (i, 0)),
        ],
        out_specs=[
            pl.BlockSpec((width, FF_BLOCK), lambda i: (0, i)), units, units,
            whole(rows, width), whole(rows, width), whole(half, width), whole(half, width),
            whole(rows, width), whole(1, width),
        ],
        scratch_shapes=[
            pltpu.VMEM((rows, width), BF16),
            pltpu.VMEM((width, rows), BF16),
            pltpu.VMEM((rows, width), F32),
            pltpu.VMEM((rows, width), F32),
        ],
        compiler_params=pltpu.CompilerParams(vmem_limit_bytes=VMEM_LIMIT),
        cost_estimate=pl.CostEstimate(flops=18_000_000_000, bytes_accessed=40_000_000, transcendentals=0),
        name="feed_forward",
    )(own, other, branch, far, gain, og_own, og_other, wgu, wd)


def unit_products(here, second, table, d_gate, d_up):
    rows, width = second.shape
    ff = d_gate.shape[1]
    q = width // RING
    piece = pl.BlockSpec((q, FF_BLOCK), lambda i: (0, i))
    units = pl.BlockSpec((rows, FF_BLOCK), lambda i: (0, i))
    return pl.pallas_call(
        unit_products_kernel,
        grid=(-(-ff // FF_BLOCK),),
        out_shape=[jax.ShapeDtypeStruct((q, ff), BF16)] * 8,
        in_specs=[
            pl.BlockSpec(memory_space=pltpu.SMEM), whole(rows, width), whole(*table.shape),
            units, units,
        ],
        out_specs=[piece] * 8,
        scratch_shapes=[pltpu.VMEM((width, rows), BF16)] * 2,
        compiler_params=pltpu.CompilerParams(vmem_limit_bytes=VMEM_LIMIT),
        cost_estimate=pl.CostEstimate(flops=7_000_000_000, bytes_accessed=16_000_000, transcendentals=0),
        name="unit_products",
    )(here, second, table, d_gate, d_up)


def attend_back_kernel(
    here_ref, mid_ref, ds_ref, far_ref, og_own_ref, og_other_ref, gain_ref, att_ref, table_ref,
    wo_ref, q_ref, k_ref, v_ref, stat_ref, place_ref, rope_ref,
    wq_ref, wkv_ref, first_t_ref, own_ref, other_ref,
    pair_ref, out_ref, d_mid_ref, d_own_ref, d_send_ref, gainsum_ref, bias_ref,
    d_branch_ref, d_all_ref, dk_ref, dv_ref,
):
    rows = q_ref.shape[0]
    half = rows // 2
    for r, og in enumerate((og_own_ref, og_other_ref)):
        a, b = pl.ds(r * half, half), pl.ds((1 - r) * half, half)
        mid = mid_ref[a, :]
        inv = lax.rsqrt(jnp.mean(mid * mid, axis=1, keepdims=True) + EPS)
        normed = mid * inv
        d = (ds_ref[a, :].astype(F32) + far_ref[b, :].astype(F32)) * gain_ref[...]
        d_mid = og[...].astype(F32) + inv * (
            d - normed * jnp.mean(d * normed, axis=1, keepdims=True)
        )
        if r == 0:
            d_mid_ref[...] = d_mid
        d_branch_ref[a, :] = d_mid.astype(BF16)
    heads = wq_ref.shape[0] // HEAD_SIZE
    scale = 0.5 / math.sqrt(HEAD_SIZE)
    rank = here_ref[0]
    keys, v_even = k_ref[...], v_ref[...]
    v_odd = rolled(v_even.astype(F32)).astype(BF16)
    low = iota((half, WIDE), 1) < HEAD_SIZE
    low_all = iota((rows, WIDE), 1) < HEAD_SIZE
    dk_ref[...] = jnp.zeros_like(dk_ref)
    dv_ref[...] = jnp.zeros_like(dv_ref)

    def back(x, cosine, sine):
        return x * cosine - rolled(x) * sine

    for r in range(2):
        part = pl.ds(r * half, half)
        ok = allowed_keys(place_ref[part, :], r * half, rank, rows)
        cosine, sine = wide_tables(rope_ref[part, :])
        d_att = nt(d_branch_ref[part, :], wo_ref[...]).astype(BF16)
        pair = None
        for h in range(heads):
            tile = h // 2
            qh = q_ref[part, h * WIDE : (h + 1) * WIDE]
            da = d_att[:, tile * WIDE : (tile + 1) * WIDE]
            if da.shape[1] < WIDE:
                da = jnp.concatenate([da, jnp.zeros_like(da)], axis=1)
            s = nt(qh, keys) * scale
            p = jnp.where(ok, jnp.exp(s - stat_ref[part, h : h + 1]), 0.0)
            dp = nt(da, v_odd if h % 2 else v_even)
            ds = (p * (dp - jnp.sum(p * dp, axis=1, keepdims=True))).astype(BF16)
            pb = p.astype(BF16)
            dk_ref[...] += tn(ds, qh)
            dv = tn(pb, da)
            dv_ref[...] += jnp.where(low_all if h % 2 == 0 else ~low_all, dv, 0.0)
            dq = back(dot(ds, keys) * (2.0 * scale), cosine, sine)
            if h % 2:
                d_all_ref[part, tile * WIDE : (tile + 1) * WIDE] = jnp.where(
                    low, pair, rolled(dq)
                ).astype(BF16)
            else:
                pair = dq
        if heads % 2:
            d_all_ref[part, (heads - 1) * HEAD_SIZE : heads * HEAD_SIZE] = pair[
                :, :HEAD_SIZE
            ].astype(BF16)
    n = heads * HEAD_SIZE
    dk = back(dk_ref[...] * (2.0 * scale), *wide_tables(rope_ref[...]))[:, :HEAD_SIZE].astype(BF16)
    dv = dv_ref[...]
    dv = (dv + rolled(dv))[:, :HEAD_SIZE].astype(BF16)
    d_all_ref[:, n : n + HEAD_SIZE] = dk
    d_all_ref[:, n + HEAD_SIZE :] = dv
    d_all = d_all_ref[...]
    pair_ref[...] = dot(first_t_ref[...], d_all).astype(BF16)
    left = permuted_rows(sent_rows(here_ref, table_ref, 3), d_branch_ref[...])
    out_ref[...] = dot(left, att_ref[...]).astype(BF16)
    bias_ref[...] = jnp.sum(d_all.astype(F32), axis=0, keepdims=True)
    total = jnp.zeros((1, own_ref.shape[1]), F32)
    for r, src in enumerate((own_ref, other_ref)):
        part = pl.ds(r * half, half)
        d_first = (
            dot(d_all_ref[part, :n], wq_ref[...])
            + dot(d_all_ref[part, n : n + HEAD_SIZE], wkv_ref[0])
            + dot(d_all_ref[part, n + HEAD_SIZE :], wkv_ref[1])
        )
        x = src[...].astype(F32)
        normed = x * lax.rsqrt(jnp.mean(x * x, axis=1, keepdims=True) + EPS)
        total = total + jnp.sum(d_first * normed, axis=0, keepdims=True)
        if r == 0:
            d_own_ref[...] = d_first
        else:
            d_send_ref[...] = d_first.astype(BF16)
    gainsum_ref[...] = total


def attend_back(
    here, mid, ds, far, og_own, og_other, gain, att, table,
    wo, q, k, v, stat, place, rope, wq, wkv, first_t, own, other,
):
    rows, width = mid.shape
    n = wq.shape[0] + 2 * HEAD_SIZE
    sds = jax.ShapeDtypeStruct
    return pl.pallas_call(
        attend_back_kernel,
        out_shape=(
            sds((width, n), BF16),
            sds((width, att.shape[1]), BF16),
            sds((rows // 2, width), F32),
            sds((rows // 2, width), F32),
            sds((rows // 2, width), BF16),
            sds((1, width), F32),
            sds((1, n), F32),
        ),
        in_specs=[pl.BlockSpec(memory_space=pltpu.SMEM)]
        + [pl.BlockSpec(memory_space=pltpu.VMEM)] * 20,
        out_specs=[pl.BlockSpec(memory_space=pltpu.VMEM)] * 7,
        scratch_shapes=[
            pltpu.VMEM((rows, width), BF16),
            pltpu.VMEM((rows, n), BF16),
            pltpu.VMEM((rows, WIDE), F32),
            pltpu.VMEM((rows, WIDE), F32),
        ],
        compiler_params=pltpu.CompilerParams(vmem_limit_bytes=VMEM_LIMIT),
        cost_estimate=pl.CostEstimate(flops=12_000_000_000, bytes_accessed=16_000_000, transcendentals=0),
        name="attention_backward",
    )(
        here, mid, ds, far, og_own, og_other, gain, att, table,
        wo, q, k, v, stat, place, rope, wq, wkv, first_t, own, other,
    )


def high_low(x):
    high = x.astype(BF16)
    return high, (x - high.astype(F32)).astype(BF16)


def put_sums(ref, row, sums):
    high, low = high_low(sums)
    ref[row : row + SUM_ROWS, :SUM_LANES] = high
    ref[row : row + SUM_ROWS, SUM_LANES : 2 * SUM_LANES] = low


def get_sums(ref, row):
    high = ref[row : row + SUM_ROWS, :SUM_LANES].astype(F32)
    return high + ref[row : row + SUM_ROWS, SUM_LANES : 2 * SUM_LANES].astype(F32)


def up_to(n, m):
    return -(-n // m) * m


def local_call(kernel, name, out_shape, *args, scratch=()):
    vmem = pl.BlockSpec(memory_space=pltpu.VMEM)
    return pl.pallas_call(
        kernel,
        out_shape=[jax.ShapeDtypeStruct(shape, dtype) for shape, dtype in out_shape],
        in_specs=[vmem] * len(args),
        out_specs=[vmem] * len(out_shape),
        scratch_shapes=list(scratch),
        compiler_params=pltpu.CompilerParams(vmem_limit_bytes=VMEM_LIMIT),
        cost_estimate=pl.CostEstimate(flops=1_000_000_000, bytes_accessed=8_000_000, transcendentals=0),
        name=name,
    )(*args)


def first_sums_kernel(
    gl_ref, gr_ref, g2_ref, ul_ref, ur_ref, u2_ref, a_ref, b_ref, gains_ref, bias_ref,
    yr_ref, yl_ref, y2_ref, xr_ref, xl_ref, x2_ref, sums_ref,
):
    h = g2_ref.shape[0] // 2
    ff = g2_ref.shape[1]
    width = gains_ref.shape[1]
    sums_ref[...] = jnp.zeros_like(sums_ref)
    rest = width - SUM_LANES
    for k in range(2):
        sums_ref[2 * k : 2 * k + 1, :] = gains_ref[k : k + 1, :SUM_LANES]
        sums_ref[2 * k + 1 : 2 * k + 2, :rest] = gains_ref[k : k + 1, SUM_LANES:]
    rest = bias_ref.shape[1] - SUM_LANES
    sums_ref[4:5, :] = bias_ref[:, :SUM_LANES]
    sums_ref[5:6, :rest] = bias_ref[:, SUM_LANES:]
    sums = sums_ref[...]
    for k, (ref, low, heard) in enumerate(((yr_ref, 0, gl_ref), (yl_ref, h, gr_ref))):
        later = g2_ref[low : low + h, :].astype(F32)
        ref[:h, :ff] = (later + heard[:h, :].astype(F32)).astype(BF16)
        n, m = a_ref.shape[1], up_to(a_ref.shape[1], 128)
        ref[:h, ff : ff + n] = a_ref[2 * k * h : (2 * k + 1) * h, :]
        ref[:h, ff + m : ff + m + n] = a_ref[(2 * k + 1) * h : (2 * k + 2) * h, :]
        put_sums(ref, h, sums)
    for k, (ref, low, heard) in enumerate(((xr_ref, 0, ul_ref), (xl_ref, h, ur_ref))):
        later = u2_ref[low : low + h, :].astype(F32)
        ref[:h, :ff] = (later + heard[:h, :].astype(F32)).astype(BF16)
        n, m = b_ref.shape[1], up_to(b_ref.shape[1], 128)
        ref[:h, ff : ff + n] = b_ref[2 * k * h : (2 * k + 1) * h, :]
        ref[:h, ff + m : ff + m + n] = b_ref[(2 * k + 1) * h : (2 * k + 2) * h, :]
    n = a_ref.shape[1]
    y2_ref[: 2 * h, :n] = a_ref[4 * h : 6 * h, :]
    high, low = high_low(sums)
    y2_ref[2 * h : 2 * h + SUM_ROWS, :SUM_LANES] = high
    y2_ref[2 * h + SUM_ROWS :, :SUM_LANES] = low
    x2_ref[:, : b_ref.shape[1]] = b_ref[4 * h : 6 * h, :]
    sums_ref[...] = high.astype(F32) + low.astype(F32)


def first_sums(gate_first, g2, up_first, u2, a, b, gains, bias):
    h, ff = g2.shape[0] // 2, g2.shape[1]
    wa, wb = up_to(a.shape[1], 128), up_to(b.shape[1], 128)
    y, x = (h + SUM_ROWS, ff + 2 * wa), (h, ff + 2 * wb)
    outs = [
        (y, BF16), (y, BF16), ((2 * h + 2 * SUM_ROWS, wa), BF16),
        (x, BF16), (x, BF16), ((2 * h, wb), BF16), ((SUM_ROWS, SUM_LANES), F32),
    ]
    return local_call(
        first_sums_kernel, "first_sums", outs, *gate_first, g2, *up_first, u2, a, b, gains, bias
    )


def second_sums_kernel(
    yl_ref, yr_ref, y2_ref, xl_ref, xr_ref, x2_ref,
    gl_ref, gr_ref, g3_ref, ul_ref, ur_ref, u3_ref, a_ref, b_ref, sums_ref,
    p0_ref, p1_ref, p2_ref, own_a_ref, q0_ref, q1_ref, q2_ref, own_b_ref, out_sums_ref,
):
    h = g3_ref.shape[0] // 2
    q = h // 2
    ff = g3_ref.shape[1]
    heard = y2_ref[2 * h : 2 * h + SUM_ROWS, :SUM_LANES].astype(F32) + y2_ref[
        2 * h + SUM_ROWS :, :SUM_LANES
    ].astype(F32)
    sums = (sums_ref[...] + heard) + (get_sums(yl_ref, h) + get_sums(yr_ref, h))
    high, low = high_low(sums)
    out_sums_ref[...] = high.astype(F32) + low.astype(F32)
    for messages, own, left, right, two, last_l, last_r, kept, mine in (
        ((p0_ref, p1_ref, p2_ref), own_a_ref, yl_ref, yr_ref, y2_ref, gl_ref, gr_ref, g3_ref, a_ref),
        ((q0_ref, q1_ref, q2_ref), own_b_ref, xl_ref, xr_ref, x2_ref, ul_ref, ur_ref, u3_ref, b_ref),
    ):
        n = mine.shape[1]
        m = up_to(n, 128)
        for k in range(2):
            first, heard = (left, last_r) if k == 0 else (right, last_l)
            part = slice(k * h, (k + 1) * h)
            big = (
                kept[part, :].astype(F32) + heard[h:, :].astype(F32) + first[:h, :ff].astype(F32)
            )
            at = ff + k * m
            small = (
                mine[6 * h + k * h : 6 * h + (k + 1) * h, :].astype(F32)
                + two[part, :n].astype(F32)
                + (left[:h, at : at + n].astype(F32) + right[:h, at : at + n].astype(F32))
            )
            for j in range(2):
                rows = slice(j * q, (j + 1) * q)
                block = 2 * k + j
                if block == 3:
                    own[:, :ff] = big[rows, :]
                    own[:, ff : ff + n] = small[rows, :]
                else:
                    messages[block][:q, :ff] = big[rows, :].astype(BF16)
                    messages[block][:q, ff : ff + n] = small[rows, :].astype(BF16)
    for ref in (p0_ref, p1_ref, p2_ref):
        put_sums(ref, q, sums)


def second_sums(y_heard, x_heard, gate_first, g3, up_first, u3, a, b, sums):
    h, ff = g3.shape[0] // 2, g3.shape[1]
    q = h // 2
    wa, wb = ff + up_to(a.shape[1], 128), ff + up_to(b.shape[1], 128)
    outs = (
        [((q + SUM_ROWS, wa), BF16)] * 3 + [((q, wa), F32)]
        + [((q, wb), BF16)] * 3 + [((q, wb), F32)]
        + [((SUM_ROWS, SUM_LANES), F32)]
    )
    return local_call(
        second_sums_kernel, "second_sums", outs,
        *y_heard, *x_heard, *gate_first, g3, *up_first, u3, a, b, sums,
    )


def third_sums_kernel(
    p0_ref, p1_ref, p2_ref, own_a_ref, q0_ref, q1_ref, q2_ref, own_b_ref, sums_ref,
    r0_ref, r1_ref, r2_ref, own_ref, out_sums_ref,
):
    q, wa = own_a_ref.shape
    r = q // RING
    sums = (sums_ref[...] + get_sums(p2_ref, q)) + (get_sums(p0_ref, q) + get_sums(p1_ref, q))
    high, low = high_low(sums)
    out_sums_ref[...] = high.astype(F32) + low.astype(F32)
    a = own_a_ref[...] + (
        p0_ref[:q, :].astype(F32) + p1_ref[:q, :].astype(F32) + p2_ref[:q, :].astype(F32)
    )
    b = own_b_ref[...] + (
        q0_ref[...].astype(F32) + q1_ref[...].astype(F32) + q2_ref[...].astype(F32)
    )
    for k, ref in enumerate((r0_ref, r1_ref, r2_ref)):
        put_sums(ref, 0, sums)
        ref[SUM_ROWS : SUM_ROWS + r, :wa] = a[k * r : (k + 1) * r, :].astype(BF16)
        ref[SUM_ROWS : SUM_ROWS + r, wa:] = b[k * r : (k + 1) * r, :].astype(BF16)
    own_ref[:r, :wa] = a[3 * r :, :]
    own_ref[:r, wa:] = b[3 * r :, :]


def third_sums(heard_a, own_a, heard_b, own_b, sums):
    r = own_a.shape[0] // RING
    n = own_a.shape[1] + own_b.shape[1]
    rows = up_to(SUM_ROWS + r, SUM_ROWS)
    outs = [((rows, n), BF16)] * 3 + [
        ((up_to(r, SUM_ROWS), n), F32), ((SUM_ROWS, SUM_LANES), F32)
    ]
    return local_call(
        third_sums_kernel, "third_sums", outs, *heard_a, own_a, *heard_b, own_b, sums
    )


def last_sums_kernel(
    r0_ref, r1_ref, r2_ref, own_ref, sums_ref,
    gate_up_ref, query_ref, pair_ref, out_ref, gain1_ref, gain2_ref, query_bias_ref, pair_bias_ref,
):
    r, ff = gate_up_ref.shape[0], gate_up_ref.shape[2]
    n = query_ref.shape[1]
    sums = (sums_ref[...] + get_sums(r2_ref, 0)) + (get_sums(r0_ref, 0) + get_sums(r1_ref, 0))
    rest = gain1_ref.shape[1] - SUM_LANES
    for k, ref in enumerate((gain1_ref, gain2_ref)):
        ref[:, :SUM_LANES] = sums[2 * k : 2 * k + 1, :]
        ref[:, SUM_LANES:] = sums[2 * k + 1 : 2 * k + 2, :rest]
    query_bias_ref[...] = sums[4:5, :n]
    pair_bias_ref[0:1, :] = sums[4:5, n : n + HEAD_SIZE]
    pair_bias_ref[1:2, :] = sums[5:6, :HEAD_SIZE]
    part = slice(SUM_ROWS, SUM_ROWS + r)
    total = own_ref[:r, :] + (
        r0_ref[part, :].astype(F32) + r1_ref[part, :].astype(F32) + r2_ref[part, :].astype(F32)
    )
    wa = ff + up_to(n + 2 * HEAD_SIZE, 128)
    gate_up_ref[:, 0, :] = total[:, :ff]
    gate_up_ref[:, 1, :] = total[:, wa : wa + ff]
    query_ref[...] = total[:, ff : ff + n]
    pair_ref[0] = total[:, ff + n : ff + n + HEAD_SIZE]
    pair_ref[1] = total[:, ff + n + HEAD_SIZE : ff + n + 2 * HEAD_SIZE]
    out_ref[...] = total[:, wa + ff : wa + ff + n]


def last_sums(heard, own, sums, ff, n, r, width):
    outs = [
        ((r, 2, ff), F32), ((r, n), F32), ((2, r, HEAD_SIZE), F32), ((r, n), F32),
        ((1, width), F32), ((1, width), F32), ((1, n), F32), ((2, HEAD_SIZE), F32),
    ]
    return local_call(last_sums_kernel, "last_sums", outs, *heard, own, sums)


def body(
    tokens,
    out_grad,
    first_gain,
    query_weight,
    query_bias,
    key_value_weight_pair,
    key_value_bias_pair,
    output_weight,
    second_gain,
    gate_up_weight,
    down_weight,
    lengths,
    group_of,
):
    own_rows, width = tokens.shape
    rows = 2 * own_rows
    tensor_rank = lax.axis_index("tensor")
    data_group = lax.axis_index(DP)
    heads = query_weight.shape[1] // HEAD_SIZE
    per_device = width // 64
    tokens_other = swap(tokens)
    og_other = swap(out_grad)
    query_weight_t = query_weight.T
    pair_weight_t = jnp.swapaxes(key_value_weight_pair, 1, 2)
    slots = jnp.arange(rows, dtype=jnp.int32) + tensor_rank * own_rows
    slots = jnp.where(slots >= rows, slots - rows, slots)
    first_slot = layout(lengths, group_of, data_group, slots)
    rope = rope_table(slots - first_slot)
    place = first_slot[:, None]
    here = jnp.stack([tensor_rank, *[lax.axis_index(axis) for axis in DP]])
    table = jnp.asarray(offset_table(per_device))
    gain1, gain2 = first_gain[None, :], second_gain[None, :]
    first_t, q, k, v, attended, stat, branch = attend(
        here, tokens, tokens_other, gain1, query_weight_t, query_bias[None, :],
        pair_weight_t, key_value_bias_pair, output_weight, place, rope, table,
    )
    branch, og_other = pinned(branch, og_other)
    down, d_gate, d_up, middle, second, res, mlp_send, ds, gain2_part = feed_forward(
        tokens, tokens_other, branch, swap(branch), gain2, out_grad, og_other,
        gate_up_weight, down_weight,
    )
    ds_far = swap(ds)
    g0, g1, g2, g3, u0, u1, u2, u3 = unit_products(here, second, table, d_gate, d_up)
    down, g0, g1, u0, u1 = pinned(down, g0, g1, u0, u1)
    down = scatter_natural(down, DP[0])
    z_axis, y_axis, x_axis = DP
    gate_first = ring_first(g0, g1, y_axis)
    up_first = ring_first(u0, u1, x_axis)
    result = (res + swap(mlp_send).astype(F32)).astype(BF16)
    pair, out, d_middle, d_own, d_send, gain1_part, bias_part = attend_back(
        here, middle, ds, ds_far, out_grad, og_other, gain2, attended, table,
        output_weight, q, k, v, stat, place, rope,
        query_weight_t, pair_weight_t, first_t, tokens, tokens_other,
    )
    gains = jnp.concatenate([gain1_part, gain2_part], axis=0)
    gains = gains + swap(gains)
    yr, yl, y2, xr, xl, x2, sums = first_sums(
        gate_first, g2, up_first, u2, pair, out, gains, bias_part
    )
    y2 = shift(y2, y_axis, 2)
    xl, y2 = pinned(xl, y2)
    y_heard = shift(yr, y_axis, 1), shift(yl, y_axis, 3), y2
    x_heard = to_others((xr, xl, x2), x_axis)
    y2, down = pinned(y_heard[2], down)
    y_heard = (*y_heard[:2], y2)
    down = scatter_natural(down, DP[1])
    p0, p1, p2, own_a, q0, q1, q2, own_b, sums = second_sums(
        y_heard, x_heard, gate_first, g3, up_first, u3, pair, out, sums
    )
    heard_a = to_others((p0, p1, p2), x_axis)
    heard_b = to_others((q0, q1, q2), y_axis)
    own_a, down = pinned(own_a, down)
    down = scatter_natural(down, DP[2])
    r0, r1, r2, own, sums = third_sums(heard_a, own_a, heard_b, own_b, sums)
    heard = to_others((r0, r1, r2), z_axis)
    n = heads * HEAD_SIZE
    ff = down.shape[1]
    gate_up, grad_query, grad_pair, grad_output, gain1, gain2, query_bias, pair_bias = last_sums(
        heard, own, sums, ff, n, per_device, width
    )

    inputs = tokens.astype(F32)
    inv_first = lax.rsqrt(jnp.mean(inputs * inputs, axis=1, keepdims=True) + EPS)
    own_normed = inputs * inv_first
    d_normed = (d_own + swap(d_send).astype(F32)) * first_gain
    grad_tokens = d_middle + inv_first * (
        d_normed - own_normed * jnp.mean(d_normed * own_normed, axis=1, keepdims=True)
    )
    return (
        result,
        grad_tokens,
        gain1[0],
        grad_query,
        query_bias[0],
        grad_pair,
        pair_bias,
        grad_output.T,
        gain2[0],
        jnp.swapaxes(gate_up, 0, 1),
        down.astype(F32).T,
    )


def solution(mesh):
    torus = Mesh(
        mesh.devices.reshape(4, 4, 4, mesh.shape["tensor"]), ("dp_0", "dp_1", "dp_2", "tensor")
    )
    placed = (
        P(DP_TENSOR, None),
        P(DP_TENSOR, None),
        P(),
        P(None, "tensor"),
        P("tensor"),
        P(None, None, "tensor"),
        P(None, "tensor"),
        P("tensor", None),
        P(),
        P(None, None, "tensor"),
        P("tensor", None),
        P(),
        P(),
    )
    return jax.shard_map(
        body,
        mesh=torus,
        in_specs=placed,
        out_specs=(
            P(DP_TENSOR, None),
            P(DP_TENSOR, None),
            P(),
            P(DP, "tensor"),
            P("tensor"),
            P(None, DP, "tensor"),
            P(None, "tensor"),
            P("tensor", DP),
            P(),
            P(None, DP, "tensor"),
            P("tensor", DP),
        ),
        check_vma=False,
    )
```

```python
import math

import jax
import jax.numpy as jnp
import numpy as np
from jax import lax
from jax.experimental import pallas as pl
from jax.experimental.pallas import tpu as pltpu
from jax.sharding import Mesh
from jax.sharding import PartitionSpec as P

HEAD_SIZE = 64
DP = ("dp_0", "dp_1", "dp_2")
DP_TENSOR = ("dp_0", "dp_1", "dp_2", "tensor")
EPS = 1e-06
THETA = 1000000.0
BF16 = jnp.bfloat16
F32 = jnp.float32
RING = 4
GATE = ((1, True), (2, False), (0, False))
UP = ((2, True), (1, False), (0, False))
SMALL = ((1, False), (2, False), (0, False))
ORDERS = (GATE, UP, SMALL)
SUM_ROWS, SUM_LANES = 8, 512
STRIDES = (16, 4, 1)


def dot(left, right):
    return jnp.dot(left, right, preferred_element_type=F32)


def contract(left, right, left_dim, right_dim):
    return lax.dot_general(
        left, right, (((left_dim,), (right_dim,)), ((), ())), preferred_element_type=F32
    )


def swap(x):
    return lax.ppermute(x, "tensor", [(0, 1), (1, 0)])


def swap_rows(x):
    half = x.shape[0] // 2
    other = swap(x)
    return jnp.concatenate([other[half:], other[:half]], axis=0)


def shift(x, axis, by):
    return lax.ppermute(x, axis, [(i, (i + by) % RING) for i in range(RING)])


def stage_order(ring, size):
    if ring:
        a, b = range(size // 2), range(size // 2, size)
        runs = ((2, a), (1, b), (2, b), (3, a), (1, a), (3, b), (0, a), (0, b))
        return [(off, row) for off, rows in runs for row in rows]
    return [(off, row) for off in (1, 3, 2, 0) for row in range(size)]


def offset_columns(order, rows_per_device):
    table = [(row,) for row in range(rows_per_device)]
    for _, ring in reversed(order):
        table = [(off, *table[row]) for off, row in stage_order(ring, len(table))]
    table = np.array(table, np.int32)
    stages = [axis for axis, _ in order]
    return [table[:, stages.index(axis)] for axis in range(3)] + [table[:, 3]]


def offset_table(rows_per_device):
    columns = [c for order in ORDERS for c in offset_columns(order, rows_per_device)]
    return np.stack(columns, axis=1)


def ring_first(send_right, send_left, axis):
    return shift(send_right, axis, 1), shift(send_left, axis, 3)


def to_others(pieces, axis):
    return [shift(piece, axis, by) for piece, by in zip(pieces, (1, 3, 2))]


def scatter_natural(x, axis):
    x = x.reshape(RING, x.shape[0] // RING, x.shape[1])
    return lax.psum_scatter(x, axis, scatter_dimension=0, tiled=True)[0]


def pinned(*xs):
    return lax.optimization_barrier(xs)


def layout(lengths, group_of, data_group, slots):
    mine = jnp.where(group_of == data_group, lengths, 0)
    ends = jnp.cumsum(mine, dtype=jnp.int32)
    past = ends[None, :] <= slots[:, None]
    return jnp.sum(jnp.where(past, mine[None, :], 0), axis=1, dtype=jnp.int32)


def rope_table(position):
    halfway = HEAD_SIZE // 2
    lane = np.arange(4 * halfway)
    freq = np.exp((lane % halfway) * (-2.0 * math.log(THETA) / HEAD_SIZE)).astype(np.float32)
    phase = np.where(lane < HEAD_SIZE, math.pi / 2, 0.0).astype(np.float32)
    return jnp.sin(position.astype(F32)[:, None] * freq[None, :] + phase)


def wide_tables(table):
    low = iota(table.shape, 1) < HEAD_SIZE
    other = rolled(table)
    return jnp.where(low, table, other), jnp.where(low, other, -table)


VMEM_LIMIT = 60 * 1024 * 1024
WIDE = 2 * HEAD_SIZE


def nt(left, right):
    return contract(left, right, 1, 1)


def tn(left, right):
    return contract(left, right, 0, 0)


def whole(*shape):
    return pl.BlockSpec(shape, lambda *_: (0,) * len(shape))


def iota(shape, dim):
    return lax.broadcasted_iota(jnp.int32, shape, dim)


def sent_rows(here_ref, table_ref, which):
    base = 4 * which
    rows = table_ref[:, base + 3 : base + 4]
    count = table_ref.shape[0] // 64
    for k, stride in enumerate(STRIDES):
        at = (table_ref[:, base + k : base + k + 1] + here_ref[1 + k]) & (RING - 1)
        rows = rows + count * stride * at
    return rows


def permuted_rows(index, x):
    width = x.shape[1]
    hot = jnp.where(index == iota((width, width), 1), 1.0, 0.0).astype(BF16)
    return nt(hot, x).astype(BF16)


def widen(heads):
    shape = (heads * WIDE, heads * HEAD_SIZE)
    row, col = iota(shape, 1), iota(shape, 0)
    inner = col % WIDE
    here = (col // WIDE) * HEAD_SIZE + inner
    half = HEAD_SIZE // 2
    e = inner - HEAD_SIZE
    turned = (col // WIDE) * HEAD_SIZE + jnp.where(e < half, e + half, e - half)
    sign = jnp.where(inner < HEAD_SIZE, 1.0, jnp.where(e < half, -1.0, 1.0))
    source = jnp.where(inner < HEAD_SIZE, here, turned)
    return jnp.where(row == source, sign, 0.0)


def rolled(x):
    return pltpu.roll(x, HEAD_SIZE, 1)


def slot_of(row, rank, rows):
    slot = row + rank * (rows // 2)
    return jnp.where(slot >= rows, slot - rows, slot)


def allowed_keys(first_slot, start, rank, rows):
    n = first_slot.shape[0]
    key = slot_of(iota((n, rows), 1), rank, rows)
    query = slot_of(iota((n, 1), 0) + start, rank, rows)
    return (key <= query) & (key >= first_slot)


def attend_kernel(
    here_ref, own_ref, other_ref, gain_ref, wq_ref, bq_ref, wkv_ref, bkv_ref, wo_ref, place_ref,
    rope_ref, table_ref,
    first_t_ref, q_ref, k_ref, v_ref, att_ref, stat_ref, branch_ref, first_ref,
):
    rows = q_ref.shape[0]
    half = rows // 2
    heads = wq_ref.shape[0] // HEAD_SIZE
    scale = 0.5 / math.sqrt(HEAD_SIZE)
    highest = lax.Precision.HIGHEST
    wide = widen(heads)
    both_last = (((1,), (1,)), ((), ()))
    wq = dot(wide.astype(BF16), wq_ref[...]).astype(BF16)
    bq = lax.dot_general(
        bq_ref[...], wide, both_last, precision=highest, preferred_element_type=F32
    )
    wide_one = widen(1)
    wk = dot(wide_one.astype(BF16), wkv_ref[0]).astype(BF16)
    bk = lax.dot_general(
        bkv_ref[0:1], wide_one, both_last, precision=highest, preferred_element_type=F32
    )
    for r, src in enumerate((own_ref, other_ref)):
        part = pl.ds(r * half, half)
        x = src[...].astype(F32)
        inv = lax.rsqrt(jnp.mean(x * x, axis=1, keepdims=True) + EPS)
        first = (x * inv * gain_ref[...]).astype(BF16)
        first_ref[part, :] = first
        cosine, sine = wide_tables(rope_ref[part, :])
        q = nt(first, wq) + bq
        for h in range(heads):
            qh = q[:, h * WIDE : (h + 1) * WIDE]
            q_ref[part, h * WIDE : (h + 1) * WIDE] = (qh * cosine + rolled(qh) * sine).astype(BF16)
        k = nt(first, wk) + bk
        k_ref[part, :] = (k * cosine + rolled(k) * sine).astype(BF16)
        v = (nt(first, wkv_ref[1]) + bkv_ref[1:2]).astype(BF16)
        v_ref[part, :] = jnp.concatenate([v, jnp.zeros_like(v)], axis=1)
    first_t_ref[...] = permuted_rows(sent_rows(here_ref, table_ref, 2), first_ref[...])
    keys, v_even = k_ref[...], v_ref[...]
    v_odd = rolled(v_even.astype(F32)).astype(BF16)
    rank = here_ref[0]
    for r in range(2):
        part = pl.ds(r * half, half)
        ok = allowed_keys(place_ref[part, :], r * half, rank, rows)
        stat = jnp.zeros((half, WIDE), F32)
        lane = iota((half, WIDE), 1)
        pair = None
        for h in range(heads):
            s = nt(q_ref[part, h * WIDE : (h + 1) * WIDE], keys) * scale
            s = jnp.where(ok, s, -1e30)
            peak = jnp.max(s, axis=1, keepdims=True)
            e = jnp.exp(s - peak)
            total = jnp.sum(e, axis=1, keepdims=True)
            p = (e * (1.0 / total)).astype(BF16)
            stat = jnp.where(lane == h, peak + jnp.log(total), stat)
            a = dot(p, v_odd if h % 2 else v_even)
            if h % 2:
                att_ref[part, (h // 2) * WIDE : (h // 2 + 1) * WIDE] = (pair + a).astype(BF16)
            else:
                pair = a
        if heads % 2:
            att_ref[part, (heads - 1) * HEAD_SIZE :] = pair[:, :HEAD_SIZE].astype(BF16)
        stat_ref[part, :] = stat
        branch_ref[part, :] = dot(att_ref[part, :], wo_ref[...]).astype(BF16)


def attend(here, own, other, gain, wq, bq, wkv, bkv, wo, place, rope, table):
    rows, width = 2 * own.shape[0], own.shape[1]
    heads = wq.shape[0] // HEAD_SIZE
    sds = jax.ShapeDtypeStruct
    outs = (
        sds((width, rows), BF16),
        sds((rows, heads * WIDE), BF16),
        sds((rows, WIDE), BF16),
        sds((rows, WIDE), BF16),
        sds((rows, heads * HEAD_SIZE), BF16),
        sds((rows, WIDE), F32),
        sds((rows, width), BF16),
    )
    return pl.pallas_call(
        attend_kernel,
        out_shape=outs,
        in_specs=[pl.BlockSpec(memory_space=pltpu.SMEM)]
        + [pl.BlockSpec(memory_space=pltpu.VMEM)] * 11,
        out_specs=[pl.BlockSpec(memory_space=pltpu.VMEM)] * 7,
        scratch_shapes=[pltpu.VMEM((rows, width), BF16)],
        compiler_params=pltpu.CompilerParams(vmem_limit_bytes=VMEM_LIMIT),
        cost_estimate=pl.CostEstimate(flops=5_000_000_000, bytes_accessed=8_000_000, transcendentals=0),
        name="attention_forward",
    )(here, own, other, gain, wq, bq, wkv, bkv, wo, place, rope, table)


def feed_forward_kernel(
    own_ref, other_ref, branch_ref, far_ref, gain_ref, og_own_ref, og_other_ref, wgu_ref, wd_ref,
    down_ref, dg_ref, du_ref, mid_ref, second_ref, res_ref, send_ref, ds_ref, gainsum_ref,
    og_ref, ot_ref, mlp_ref, acc_ref,
):
    step = pl.program_id(0)
    last = pl.num_programs(0) - 1
    half, width = own_ref.shape

    @pl.when(step == 0)
    def _():
        for r, tok in enumerate((own_ref, other_ref)):
            a, b = pl.ds(r * half, half), pl.ds((1 - r) * half, half)
            mid = tok[...].astype(F32) + (
                branch_ref[a, :].astype(F32) + far_ref[b, :].astype(F32)
            )
            mid_ref[a, :] = mid
            inv = lax.rsqrt(jnp.mean(mid * mid, axis=1, keepdims=True) + EPS)
            second_ref[a, :] = (mid * inv * gain_ref[...]).astype(BF16)
        for r, og in enumerate((og_own_ref, og_other_ref)):
            og_ref[r * half : (r + 1) * half, :] = og[...]
            ot_ref[:, r * half : (r + 1) * half] = og[...].T
        mlp_ref[...] = jnp.zeros_like(mlp_ref)
        acc_ref[...] = jnp.zeros_like(acc_ref)

    def units(n):
        wg, wu, wd = wgu_ref[0, :, :n], wgu_ref[1, :, :n], wd_ref[:n, :]
        second = second_ref[...]
        gate, up = dot(second, wg), dot(second, wu)
        d_hidden = nt(og_ref[...], wd)
        sigmoid = 1.0 / (1.0 + jnp.exp(-gate))
        act = gate * sigmoid
        hidden = (act * up).astype(BF16)
        d_gate = (d_hidden * up * (sigmoid * (1.0 + gate * (1.0 - sigmoid)))).astype(BF16)
        d_up = (d_hidden * act).astype(BF16)
        dg_ref[:, :n] = d_gate
        du_ref[:, :n] = d_up
        down_ref[:, :n] = dot(ot_ref[...], hidden).astype(BF16)
        mlp_ref[...] += dot(hidden, wd)
        acc_ref[...] += nt(d_gate, wg) + nt(d_up, wu)

    full = wd_ref.shape[0]
    tail = FF_LOCAL % full

    @pl.when(step < last)
    def _():
        units(full)

    @pl.when(step == last)
    def _():
        units(tail or full)
        res_ref[...] = mid_ref[:half, :] + mlp_ref[:half, :]
        send_ref[...] = mlp_ref[half:, :].astype(BF16)
        ds = acc_ref[...]
        ds_ref[...] = ds.astype(BF16)
        mid = mid_ref[...]
        normed = mid * lax.rsqrt(jnp.mean(mid * mid, axis=1, keepdims=True) + EPS)
        gainsum_ref[...] = jnp.sum(ds * normed, axis=0, keepdims=True)


def unit_products_kernel(
    here_ref, second_ref, table_ref, dg_ref, du_ref,
    g0_ref, g1_ref, g2_ref, g3_ref, u0_ref, u1_ref, u2_ref, u3_ref,
    gt_ref, ut_ref,
):
    quarter = g0_ref.shape[0]

    @pl.when(pl.program_id(0) == 0)
    def _():
        gt_ref[...] = permuted_rows(sent_rows(here_ref, table_ref, 0), second_ref[...])
        ut_ref[...] = permuted_rows(sent_rows(here_ref, table_ref, 1), second_ref[...])

    for k, ref in enumerate((g0_ref, g1_ref, g2_ref, g3_ref)):
        ref[...] = dot(gt_ref[k * quarter : (k + 1) * quarter, :], dg_ref[...]).astype(BF16)
    for k, ref in enumerate((u0_ref, u1_ref, u2_ref, u3_ref)):
        ref[...] = dot(ut_ref[k * quarter : (k + 1) * quarter, :], du_ref[...]).astype(BF16)


FF_LOCAL = 2432
FF_BLOCK = 512


def feed_forward(own, other, branch, far, gain, og_own, og_other, wgu, wd):
    half, width = own.shape
    rows = 2 * half
    ff = wd.shape[0]
    sds = jax.ShapeDtypeStruct
    units = pl.BlockSpec((rows, FF_BLOCK), lambda i: (0, i))
    return pl.pallas_call(
        feed_forward_kernel,
        grid=(-(-ff // FF_BLOCK),),
        out_shape=[
            sds((width, ff), BF16),
            sds((rows, ff), BF16),
            sds((rows, ff), BF16),
            sds((rows, width), F32),
            sds((rows, width), BF16),
            sds((half, width), F32),
            sds((half, width), BF16),
            sds((rows, width), BF16),
            sds((1, width), F32),
        ],
        in_specs=[
            whole(half, width), whole(half, width), whole(rows, width), whole(rows, width),
            whole(1, width), whole(half, width), whole(half, width),
            pl.BlockSpec((2, width, FF_BLOCK), lambda i: (0, 0, i)),
            pl.BlockSpec((FF_BLOCK, width), lambda i: (i, 0)),
        ],
        out_specs=[
            pl.BlockSpec((width, FF_BLOCK), lambda i: (0, i)), units, units,
            whole(rows, width), whole(rows, width), whole(half, width), whole(half, width),
            whole(rows, width), whole(1, width),
        ],
        scratch_shapes=[
            pltpu.VMEM((rows, width), BF16),
            pltpu.VMEM((width, rows), BF16),
            pltpu.VMEM((rows, width), F32),
            pltpu.VMEM((rows, width), F32),
        ],
        compiler_params=pltpu.CompilerParams(vmem_limit_bytes=VMEM_LIMIT),
        cost_estimate=pl.CostEstimate(flops=18_000_000_000, bytes_accessed=40_000_000, transcendentals=0),
        name="feed_forward",
    )(own, other, branch, far, gain, og_own, og_other, wgu, wd)


def unit_products(here, second, table, d_gate, d_up):
    rows, width = second.shape
    ff = d_gate.shape[1]
    q = width // RING
    piece = pl.BlockSpec((q, FF_BLOCK), lambda i: (0, i))
    units = pl.BlockSpec((rows, FF_BLOCK), lambda i: (0, i))
    return pl.pallas_call(
        unit_products_kernel,
        grid=(-(-ff // FF_BLOCK),),
        out_shape=[jax.ShapeDtypeStruct((q, ff), BF16)] * 8,
        in_specs=[
            pl.BlockSpec(memory_space=pltpu.SMEM), whole(rows, width), whole(*table.shape),
            units, units,
        ],
        out_specs=[piece] * 8,
        scratch_shapes=[pltpu.VMEM((width, rows), BF16)] * 2,
        compiler_params=pltpu.CompilerParams(vmem_limit_bytes=VMEM_LIMIT),
        cost_estimate=pl.CostEstimate(flops=7_000_000_000, bytes_accessed=16_000_000, transcendentals=0),
        name="unit_products",
    )(here, second, table, d_gate, d_up)


def attend_back_kernel(
    here_ref, mid_ref, ds_ref, far_ref, og_own_ref, og_other_ref, gain_ref, att_ref, table_ref,
    wo_ref, q_ref, k_ref, v_ref, stat_ref, place_ref, rope_ref,
    wq_ref, wkv_ref, first_t_ref, own_ref, other_ref,
    block_ref, d_mid_ref, d_own_ref, d_send_ref, gainsum_ref, bias_ref,
    d_branch_ref, d_all_ref, dk_ref, dv_ref,
):
    rows = q_ref.shape[0]
    half = rows // 2
    for r, og in enumerate((og_own_ref, og_other_ref)):
        a, b = pl.ds(r * half, half), pl.ds((1 - r) * half, half)
        mid = mid_ref[a, :]
        inv = lax.rsqrt(jnp.mean(mid * mid, axis=1, keepdims=True) + EPS)
        normed = mid * inv
        d = (ds_ref[a, :].astype(F32) + far_ref[b, :].astype(F32)) * gain_ref[...]
        d_mid = og[...].astype(F32) + inv * (
            d - normed * jnp.mean(d * normed, axis=1, keepdims=True)
        )
        if r == 0:
            d_mid_ref[...] = d_mid
        d_branch_ref[a, :] = d_mid.astype(BF16)
    heads = wq_ref.shape[0] // HEAD_SIZE
    scale = 0.5 / math.sqrt(HEAD_SIZE)
    rank = here_ref[0]
    keys, v_even = k_ref[...], v_ref[...]
    v_odd = rolled(v_even.astype(F32)).astype(BF16)
    low = iota((half, WIDE), 1) < HEAD_SIZE
    low_all = iota((rows, WIDE), 1) < HEAD_SIZE
    dk_ref[...] = jnp.zeros_like(dk_ref)
    dv_ref[...] = jnp.zeros_like(dv_ref)

    def back(x, cosine, sine):
        return x * cosine - rolled(x) * sine

    for r in range(2):
        part = pl.ds(r * half, half)
        ok = allowed_keys(place_ref[part, :], r * half, rank, rows)
        cosine, sine = wide_tables(rope_ref[part, :])
        d_att = nt(d_branch_ref[part, :], wo_ref[...]).astype(BF16)
        pair = None
        for h in range(heads):
            tile = h // 2
            qh = q_ref[part, h * WIDE : (h + 1) * WIDE]
            da = d_att[:, tile * WIDE : (tile + 1) * WIDE]
            if da.shape[1] < WIDE:
                da = jnp.concatenate([da, jnp.zeros_like(da)], axis=1)
            s = nt(qh, keys) * scale
            p = jnp.where(ok, jnp.exp(s - stat_ref[part, h : h + 1]), 0.0)
            dp = nt(da, v_odd if h % 2 else v_even)
            ds = (p * (dp - jnp.sum(p * dp, axis=1, keepdims=True))).astype(BF16)
            pb = p.astype(BF16)
            dk_ref[...] += tn(ds, qh)
            dv = tn(pb, da)
            dv_ref[...] += jnp.where(low_all if h % 2 == 0 else ~low_all, dv, 0.0)
            dq = back(dot(ds, keys) * (2.0 * scale), cosine, sine)
            if h % 2:
                d_all_ref[part, tile * WIDE : (tile + 1) * WIDE] = jnp.where(
                    low, pair, rolled(dq)
                ).astype(BF16)
            else:
                pair = dq
        if heads % 2:
            d_all_ref[part, (heads - 1) * HEAD_SIZE : heads * HEAD_SIZE] = pair[
                :, :HEAD_SIZE
            ].astype(BF16)
    n = heads * HEAD_SIZE
    dk = back(dk_ref[...] * (2.0 * scale), *wide_tables(rope_ref[...]))[:, :HEAD_SIZE].astype(BF16)
    dv = dv_ref[...]
    dv = (dv + rolled(dv))[:, :HEAD_SIZE].astype(BF16)
    d_all_ref[:, n : n + HEAD_SIZE] = dk
    d_all_ref[:, n + HEAD_SIZE :] = dv
    d_all = d_all_ref[...]
    m = n + 2 * HEAD_SIZE
    block_ref[:, :m] = dot(first_t_ref[...], d_all).astype(BF16)
    left = permuted_rows(sent_rows(here_ref, table_ref, 2), d_branch_ref[...])
    block_ref[:, m:] = dot(left, att_ref[...]).astype(BF16)
    bias_ref[...] = jnp.sum(d_all.astype(F32), axis=0, keepdims=True)
    total = jnp.zeros((1, own_ref.shape[1]), F32)
    for r, src in enumerate((own_ref, other_ref)):
        part = pl.ds(r * half, half)
        d_first = (
            dot(d_all_ref[part, :n], wq_ref[...])
            + dot(d_all_ref[part, n : n + HEAD_SIZE], wkv_ref[0])
            + dot(d_all_ref[part, n + HEAD_SIZE :], wkv_ref[1])
        )
        x = src[...].astype(F32)
        normed = x * lax.rsqrt(jnp.mean(x * x, axis=1, keepdims=True) + EPS)
        total = total + jnp.sum(d_first * normed, axis=0, keepdims=True)
        if r == 0:
            d_own_ref[...] = d_first
        else:
            d_send_ref[...] = d_first.astype(BF16)
    gainsum_ref[...] = total


def attend_back(
    here, mid, ds, far, og_own, og_other, gain, att, table,
    wo, q, k, v, stat, place, rope, wq, wkv, first_t, own, other,
):
    rows, width = mid.shape
    n = wq.shape[0] + 2 * HEAD_SIZE
    sds = jax.ShapeDtypeStruct
    return pl.pallas_call(
        attend_back_kernel,
        out_shape=(
            sds((width, n + att.shape[1]), BF16),
            sds((rows // 2, width), F32),
            sds((rows // 2, width), F32),
            sds((rows // 2, width), BF16),
            sds((1, width), F32),
            sds((1, n), F32),
        ),
        in_specs=[pl.BlockSpec(memory_space=pltpu.SMEM)]
        + [pl.BlockSpec(memory_space=pltpu.VMEM)] * 20,
        out_specs=[pl.BlockSpec(memory_space=pltpu.VMEM)] * 6,
        scratch_shapes=[
            pltpu.VMEM((rows, width), BF16),
            pltpu.VMEM((rows, n), BF16),
            pltpu.VMEM((rows, WIDE), F32),
            pltpu.VMEM((rows, WIDE), F32),
        ],
        compiler_params=pltpu.CompilerParams(vmem_limit_bytes=VMEM_LIMIT),
        cost_estimate=pl.CostEstimate(flops=12_000_000_000, bytes_accessed=16_000_000, transcendentals=0),
        name="attention_backward",
    )(
        here, mid, ds, far, og_own, og_other, gain, att, table,
        wo, q, k, v, stat, place, rope, wq, wkv, first_t, own, other,
    )


def high_low(x):
    high = x.astype(BF16)
    return high, (x - high.astype(F32)).astype(BF16)


def put_sums(ref, row, sums):
    high, low = high_low(sums)
    ref[row : row + SUM_ROWS, :SUM_LANES] = high
    ref[row : row + SUM_ROWS, SUM_LANES : 2 * SUM_LANES] = low


def get_sums(ref, row):
    high = ref[row : row + SUM_ROWS, :SUM_LANES].astype(F32)
    return high + ref[row : row + SUM_ROWS, SUM_LANES : 2 * SUM_LANES].astype(F32)


def up_to(n, m):
    return -(-n // m) * m


def local_call(kernel, name, out_shape, *args, scratch=()):
    vmem = pl.BlockSpec(memory_space=pltpu.VMEM)
    return pl.pallas_call(
        kernel,
        out_shape=[jax.ShapeDtypeStruct(shape, dtype) for shape, dtype in out_shape],
        in_specs=[vmem] * len(args),
        out_specs=[vmem] * len(out_shape),
        scratch_shapes=list(scratch),
        compiler_params=pltpu.CompilerParams(vmem_limit_bytes=VMEM_LIMIT),
        cost_estimate=pl.CostEstimate(flops=1_000_000_000, bytes_accessed=8_000_000, transcendentals=0),
        name=name,
    )(*args)


def first_sums_kernel(
    gl_ref, gr_ref, g2_ref, ul_ref, ur_ref, u2_ref, a_ref, gains_ref, bias_ref,
    yr_ref, yl_ref, y2_ref, xr_ref, xl_ref, sums_ref,
):
    h = g2_ref.shape[0] // 2
    ff = g2_ref.shape[1]
    width = gains_ref.shape[1]
    sums_ref[...] = jnp.zeros_like(sums_ref)
    rest = width - SUM_LANES
    for k in range(2):
        sums_ref[2 * k : 2 * k + 1, :] = gains_ref[k : k + 1, :SUM_LANES]
        sums_ref[2 * k + 1 : 2 * k + 2, :rest] = gains_ref[k : k + 1, SUM_LANES:]
    rest = bias_ref.shape[1] - SUM_LANES
    sums_ref[4:5, :] = bias_ref[:, :SUM_LANES]
    sums_ref[5:6, :rest] = bias_ref[:, SUM_LANES:]
    sums = sums_ref[...]
    for k, (ref, low, heard) in enumerate(((yr_ref, 0, gl_ref), (yl_ref, h, gr_ref))):
        later = g2_ref[low : low + h, :].astype(F32)
        ref[:h, :ff] = (later + heard[:h, :].astype(F32)).astype(BF16)
        n = a_ref.shape[1]
        ref[:h, ff : ff + n] = a_ref[2 * k * h : (2 * k + 1) * h, :]
        ref[:h, ff + n :] = a_ref[(2 * k + 1) * h : (2 * k + 2) * h, :]
        put_sums(ref, h, sums)
    for k, (ref, low, heard) in enumerate(((xr_ref, 0, ul_ref), (xl_ref, h, ur_ref))):
        later = u2_ref[low : low + h, :].astype(F32)
        ref[...] = (later + heard[:h, :].astype(F32)).astype(BF16)
    y2_ref[: 2 * h, :] = a_ref[4 * h : 6 * h, :]
    put_sums(y2_ref, 2 * h, sums)
    high, low = high_low(sums)
    sums_ref[...] = high.astype(F32) + low.astype(F32)


def first_sums(gate_first, g2, up_first, u2, a, gains, bias):
    h, ff = g2.shape[0] // 2, g2.shape[1]
    n = a.shape[1]
    y, x = (h + SUM_ROWS, ff + 2 * n), (h, ff)
    outs = [
        (y, BF16), (y, BF16), ((2 * h + SUM_ROWS, n), BF16),
        (x, BF16), (x, BF16), ((SUM_ROWS, SUM_LANES), F32),
    ]
    return local_call(
        first_sums_kernel, "first_sums", outs, *gate_first, g2, *up_first, u2, a, gains, bias
    )


def second_sums_kernel(
    yl_ref, yr_ref, y2_ref, xl_ref, xr_ref,
    gl_ref, gr_ref, g3_ref, ul_ref, ur_ref, u3_ref, mine_ref, sums_ref,
    p0_ref, p1_ref, p2_ref, own_a_ref, q0_ref, q1_ref, q2_ref, own_b_ref, out_sums_ref,
):
    h = g3_ref.shape[0] // 2
    q = h // 2
    ff = g3_ref.shape[1]
    n = mine_ref.shape[1]
    sums = (sums_ref[...] + get_sums(y2_ref, 2 * h)) + (get_sums(yl_ref, h) + get_sums(yr_ref, h))
    high, low = high_low(sums)
    out_sums_ref[...] = high.astype(F32) + low.astype(F32)
    groups = (
        ((p0_ref, p1_ref, p2_ref, own_a_ref), (gr_ref, yl_ref), (gl_ref, yr_ref), g3_ref),
        ((q0_ref, q1_ref, q2_ref, own_b_ref), (ur_ref, xl_ref), (ul_ref, xr_ref), u3_ref),
    )
    for refs, *heard, kept in groups:
        for k, (first, second) in enumerate(heard):
            big = (
                kept[k * h : (k + 1) * h, :].astype(F32)
                + first[h:, :].astype(F32)
                + second[:h, :ff].astype(F32)
            )
            for j in range(2):
                ref = refs[2 * k + j]
                ref[:q, :ff] = big[j * q : (j + 1) * q, :].astype(ref.dtype)
    for k in range(2):
        at = slice(ff + k * n, ff + (k + 1) * n)
        part = slice(k * h, (k + 1) * h)
        small = (
            mine_ref[6 * h + k * h : 6 * h + (k + 1) * h, :].astype(F32)
            + y2_ref[part, :].astype(F32)
            + (yl_ref[:h, at].astype(F32) + yr_ref[:h, at].astype(F32))
        )
        for j in range(2):
            ref = (p0_ref, p1_ref, p2_ref, own_a_ref)[2 * k + j]
            ref[:q, ff:] = small[j * q : (j + 1) * q, :].astype(ref.dtype)
    for ref in (p0_ref, p1_ref, p2_ref):
        put_sums(ref, q, sums)


def second_sums(y_heard, x_heard, gate_first, g3, up_first, u3, mine, sums):
    h, ff = g3.shape[0] // 2, g3.shape[1]
    q, n = h // 2, ff + mine.shape[1]
    outs = (
        [((q + SUM_ROWS, n), BF16)] * 3 + [((q, n), F32)]
        + [((q, ff), BF16)] * 3 + [((q, ff), F32)]
        + [((SUM_ROWS, SUM_LANES), F32)]
    )
    return local_call(
        second_sums_kernel, "second_sums", outs,
        *y_heard, *x_heard, *gate_first, g3, *up_first, u3, mine, sums,
    )


def third_sums_kernel(
    p0_ref, p1_ref, p2_ref, own_a_ref, q0_ref, q1_ref, q2_ref, own_b_ref, sums_ref,
    r0_ref, r1_ref, r2_ref, own_ref, out_sums_ref,
):
    q, wa = own_a_ref.shape
    r = q // RING
    sums = (sums_ref[...] + get_sums(p2_ref, q)) + (get_sums(p0_ref, q) + get_sums(p1_ref, q))
    high, low = high_low(sums)
    out_sums_ref[...] = high.astype(F32) + low.astype(F32)
    a = own_a_ref[...] + (
        p0_ref[:q, :].astype(F32) + p1_ref[:q, :].astype(F32) + p2_ref[:q, :].astype(F32)
    )
    b = own_b_ref[...] + (
        q0_ref[...].astype(F32) + q1_ref[...].astype(F32) + q2_ref[...].astype(F32)
    )
    for k, ref in enumerate((r0_ref, r1_ref, r2_ref)):
        put_sums(ref, 0, sums)
        ref[SUM_ROWS : SUM_ROWS + r, :wa] = a[k * r : (k + 1) * r, :].astype(BF16)
        ref[SUM_ROWS : SUM_ROWS + r, wa:] = b[k * r : (k + 1) * r, :].astype(BF16)
    own_ref[:r, :wa] = a[3 * r :, :]
    own_ref[:r, wa:] = b[3 * r :, :]


def third_sums(heard_a, own_a, heard_b, own_b, sums):
    r = own_a.shape[0] // RING
    n = own_a.shape[1] + own_b.shape[1]
    rows = up_to(SUM_ROWS + r, SUM_ROWS)
    outs = [((rows, n), BF16)] * 3 + [
        ((up_to(r, SUM_ROWS), n), F32), ((SUM_ROWS, SUM_LANES), F32)
    ]
    return local_call(
        third_sums_kernel, "third_sums", outs, *heard_a, own_a, *heard_b, own_b, sums
    )


def last_sums_kernel(
    r0_ref, r1_ref, r2_ref, own_ref, sums_ref,
    gate_up_ref, query_ref, pair_ref, out_ref, gains_ref, query_bias_ref, pair_bias_ref,
):
    r, ff = gate_up_ref.shape[0], gate_up_ref.shape[2]
    n = query_ref.shape[1]
    sums = (sums_ref[...] + get_sums(r2_ref, 0)) + (get_sums(r0_ref, 0) + get_sums(r1_ref, 0))
    rest = gains_ref.shape[1] - SUM_LANES
    for k in range(2):
        gains_ref[k : k + 1, :SUM_LANES] = sums[2 * k : 2 * k + 1, :]
        gains_ref[k : k + 1, SUM_LANES:] = sums[2 * k + 1 : 2 * k + 2, :rest]
    query_bias_ref[...] = sums[4:5, :n]
    pair_bias_ref[0:1, :] = sums[4:5, n : n + HEAD_SIZE]
    pair_bias_ref[1:2, :] = sums[5:6, :HEAD_SIZE]
    part = slice(SUM_ROWS, SUM_ROWS + r)
    total = own_ref[:r, :] + (
        r0_ref[part, :].astype(F32) + r1_ref[part, :].astype(F32) + r2_ref[part, :].astype(F32)
    )
    m = ff + n + 2 * HEAD_SIZE
    gate_up_ref[:, 0, :] = total[:, :ff]
    gate_up_ref[:, 1, :] = total[:, m + n :]
    query_ref[...] = total[:, ff : ff + n]
    pair_ref[:, 0, :] = total[:, ff + n : ff + n + HEAD_SIZE]
    pair_ref[:, 1, :] = total[:, ff + n + HEAD_SIZE : ff + n + 2 * HEAD_SIZE]
    out_ref[...] = total[:, m : m + n]


def last_sums(heard, own, sums, ff, n, r, width):
    outs = [
        ((r, 2, ff), F32), ((r, n), F32), ((r, 2, HEAD_SIZE), F32), ((r, n), F32),
        ((2, width), F32), ((1, n), F32), ((2, HEAD_SIZE), F32),
    ]
    return local_call(last_sums_kernel, "last_sums", outs, *heard, own, sums)


def body(
    tokens,
    out_grad,
    first_gain,
    query_weight,
    query_bias,
    key_value_weight_pair,
    key_value_bias_pair,
    output_weight,
    second_gain,
    gate_up_weight,
    down_weight,
    lengths,
    group_of,
):
    own_rows, width = tokens.shape
    rows = 2 * own_rows
    tensor_rank = lax.axis_index("tensor")
    data_group = lax.axis_index(DP)
    heads = query_weight.shape[1] // HEAD_SIZE
    per_device = width // 64
    tokens_other = swap(tokens)
    og_other = swap(out_grad)
    query_weight_t = query_weight.T
    pair_weight_t = jnp.swapaxes(key_value_weight_pair, 1, 2)
    slots = jnp.arange(rows, dtype=jnp.int32) + tensor_rank * own_rows
    slots = jnp.where(slots >= rows, slots - rows, slots)
    first_slot = layout(lengths, group_of, data_group, slots)
    rope = rope_table(slots - first_slot)
    place = first_slot[:, None]
    here = jnp.stack([tensor_rank, *[lax.axis_index(axis) for axis in DP]])
    table = jnp.asarray(offset_table(per_device))
    gain1, gain2 = first_gain[None, :], second_gain[None, :]
    first_t, q, k, v, attended, stat, branch = attend(
        here, tokens, tokens_other, gain1, query_weight_t, query_bias[None, :],
        pair_weight_t, key_value_bias_pair, output_weight, place, rope, table,
    )
    branch, og_other = pinned(branch, og_other)
    down, d_gate, d_up, middle, second, res, mlp_send, ds, gain2_part = feed_forward(
        tokens, tokens_other, branch, swap(branch), gain2, out_grad, og_other,
        gate_up_weight, down_weight,
    )
    ds_far = swap(ds)
    g0, g1, g2, g3, u0, u1, u2, u3 = unit_products(here, second, table, d_gate, d_up)
    down, g0, g1, u0, u1 = pinned(down, g0, g1, u0, u1)
    down = scatter_natural(down, DP[0])
    z_axis, y_axis, x_axis = DP
    gate_first = ring_first(g0, g1, y_axis)
    up_first = ring_first(u0, u1, x_axis)
    result = (res + swap(mlp_send).astype(F32)).astype(BF16)
    block, d_middle, d_own, d_send, gain1_part, bias_part = attend_back(
        here, middle, ds, ds_far, out_grad, og_other, gain2, attended, table,
        output_weight, q, k, v, stat, place, rope,
        query_weight_t, pair_weight_t, first_t, tokens, tokens_other,
    )
    gains = jnp.concatenate([gain1_part, gain2_part], axis=0)
    gains = gains + swap(gains)
    yr, yl, y2, xr, xl, sums = first_sums(
        gate_first, g2, up_first, u2, block, gains, bias_part
    )
    y_heard = to_others((yr, yl, y2), y_axis)
    x_heard = ring_first(xr, xl, x_axis)
    down = scatter_natural(down, DP[1])
    p0, p1, p2, own_a, q0, q1, q2, own_b, sums = second_sums(
        y_heard, x_heard, gate_first, g3, up_first, u3, block, sums
    )
    heard_a = to_others((p0, p1, p2), x_axis)
    heard_b = to_others((q0, q1, q2), y_axis)
    down = scatter_natural(down, DP[2])
    r0, r1, r2, own, sums = third_sums(heard_a, own_a, heard_b, own_b, sums)
    heard = to_others((r0, r1, r2), z_axis)
    n = heads * HEAD_SIZE
    ff = down.shape[1]
    gate_up, grad_query, grad_pair, grad_output, gains, query_bias, pair_bias = last_sums(
        heard, own, sums, ff, n, per_device, width
    )

    inputs = tokens.astype(F32)
    inv_first = lax.rsqrt(jnp.mean(inputs * inputs, axis=1, keepdims=True) + EPS)
    own_normed = inputs * inv_first
    d_normed = (d_own + swap(d_send).astype(F32)) * first_gain
    grad_tokens = d_middle + inv_first * (
        d_normed - own_normed * jnp.mean(d_normed * own_normed, axis=1, keepdims=True)
    )
    return (
        result,
        grad_tokens,
        gains[0],
        grad_query,
        query_bias[0],
        jnp.swapaxes(grad_pair, 0, 1),
        pair_bias,
        grad_output.T,
        gains[1],
        jnp.swapaxes(gate_up, 0, 1),
        down.astype(F32).T,
    )


def solution(mesh):
    torus = Mesh(
        mesh.devices.reshape(4, 4, 4, mesh.shape["tensor"]), ("dp_0", "dp_1", "dp_2", "tensor")
    )
    placed = (
        P(DP_TENSOR, None),
        P(DP_TENSOR, None),
        P(),
        P(None, "tensor"),
        P("tensor"),
        P(None, None, "tensor"),
        P(None, "tensor"),
        P("tensor", None),
        P(),
        P(None, None, "tensor"),
        P("tensor", None),
        P(),
        P(),
    )
    return jax.shard_map(
        body,
        mesh=torus,
        in_specs=placed,
        out_specs=(
            P(DP_TENSOR, None),
            P(DP_TENSOR, None),
            P(),
            P(DP, "tensor"),
            P("tensor"),
            P(None, DP, "tensor"),
            P(None, "tensor"),
            P("tensor", DP),
            P(),
            P(None, DP, "tensor"),
            P("tensor", DP),
        ),
        check_vma=False,
    )
```

```python
import math

import jax
import jax.numpy as jnp
import numpy as np
from jax import lax
from jax.experimental import pallas as pl
from jax.experimental.pallas import tpu as pltpu
from jax.sharding import Mesh
from jax.sharding import PartitionSpec as P

HEAD_SIZE = 64
DP = ("dp_0", "dp_1", "dp_2")
DP_TENSOR = ("dp_0", "dp_1", "dp_2", "tensor")
EPS = 1e-06
THETA = 1000000.0
BF16 = jnp.bfloat16
F32 = jnp.float32
RING = 4
GATE = ((1, True), (2, False), (0, False))
UP = ((2, True), (1, False), (0, False))
SMALL = ((1, False), (2, False), (0, False))
ORDERS = (GATE, UP, SMALL)
SUM_ROWS, SUM_LANES = 8, 512
STRIDES = (16, 4, 1)


def dot(left, right):
    return jnp.dot(left, right, preferred_element_type=F32)


def contract(left, right, left_dim, right_dim):
    return lax.dot_general(
        left, right, (((left_dim,), (right_dim,)), ((), ())), preferred_element_type=F32
    )


def swap(x):
    return lax.ppermute(x, "tensor", [(0, 1), (1, 0)])


def swap_rows(x):
    half = x.shape[0] // 2
    other = swap(x)
    return jnp.concatenate([other[half:], other[:half]], axis=0)


def shift(x, axis, by):
    return lax.ppermute(x, axis, [(i, (i + by) % RING) for i in range(RING)])


def stage_order(ring, size):
    if ring:
        a, b = range(size // 2), range(size // 2, size)
        runs = ((2, a), (1, b), (2, b), (3, a), (1, a), (3, b), (0, a), (0, b))
        return [(off, row) for off, rows in runs for row in rows]
    return [(off, row) for off in (1, 3, 2, 0) for row in range(size)]


def offset_columns(order, rows_per_device):
    table = [(row,) for row in range(rows_per_device)]
    for _, ring in reversed(order):
        table = [(off, *table[row]) for off, row in stage_order(ring, len(table))]
    table = np.array(table, np.int32)
    stages = [axis for axis, _ in order]
    return [table[:, stages.index(axis)] for axis in range(3)] + [table[:, 3]]


def offset_table(rows_per_device):
    columns = [c for order in ORDERS for c in offset_columns(order, rows_per_device)]
    return np.stack(columns, axis=1)


def ring_first(send_right, send_left, axis):
    return shift(send_right, axis, 1), shift(send_left, axis, 3)


def to_others(pieces, axis):
    return [shift(piece, axis, by) for piece, by in zip(pieces, (1, 3, 2))]


def scatter_natural(x, axis):
    x = x.reshape(RING, x.shape[0] // RING, x.shape[1])
    return lax.psum_scatter(x, axis, scatter_dimension=0, tiled=True)[0]


def pinned(*xs):
    return lax.optimization_barrier(xs)


def layout(lengths, group_of, data_group, slots):
    mine = jnp.where(group_of == data_group, lengths, 0)
    ends = jnp.cumsum(mine, dtype=jnp.int32)
    past = ends[None, :] <= slots[:, None]
    return jnp.sum(jnp.where(past, mine[None, :], 0), axis=1, dtype=jnp.int32)


def rope_table(position):
    halfway = HEAD_SIZE // 2
    lane = np.arange(4 * halfway)
    freq = np.exp((lane % halfway) * (-2.0 * math.log(THETA) / HEAD_SIZE)).astype(np.float32)
    phase = np.where(lane < HEAD_SIZE, math.pi / 2, 0.0).astype(np.float32)
    return jnp.sin(position.astype(F32)[:, None] * freq[None, :] + phase)


def wide_tables(table):
    low = iota(table.shape, 1) < HEAD_SIZE
    other = rolled(table)
    return jnp.where(low, table, other), jnp.where(low, other, -table)


VMEM_LIMIT = 60 * 1024 * 1024
WIDE = 2 * HEAD_SIZE


def nt(left, right):
    return contract(left, right, 1, 1)


def tn(left, right):
    return contract(left, right, 0, 0)


def whole(*shape):
    return pl.BlockSpec(shape, lambda *_: (0,) * len(shape))


def iota(shape, dim):
    return lax.broadcasted_iota(jnp.int32, shape, dim)


def sent_rows(here_ref, table_ref, which):
    base = 4 * which
    rows = table_ref[:, base + 3 : base + 4]
    count = table_ref.shape[0] // 64
    for k, stride in enumerate(STRIDES):
        at = (table_ref[:, base + k : base + k + 1] + here_ref[1 + k]) & (RING - 1)
        rows = rows + count * stride * at
    return rows


def permuted_rows(index, x):
    width = x.shape[1]
    hot = jnp.where(index == iota((width, width), 1), 1.0, 0.0).astype(BF16)
    return nt(hot, x).astype(BF16)


def widen(heads):
    shape = (heads * WIDE, heads * HEAD_SIZE)
    row, col = iota(shape, 1), iota(shape, 0)
    inner = col % WIDE
    here = (col // WIDE) * HEAD_SIZE + inner
    half = HEAD_SIZE // 2
    e = inner - HEAD_SIZE
    turned = (col // WIDE) * HEAD_SIZE + jnp.where(e < half, e + half, e - half)
    sign = jnp.where(inner < HEAD_SIZE, 1.0, jnp.where(e < half, -1.0, 1.0))
    source = jnp.where(inner < HEAD_SIZE, here, turned)
    return jnp.where(row == source, sign, 0.0)


def rolled(x):
    return pltpu.roll(x, HEAD_SIZE, 1)


def slot_of(row, rank, rows):
    slot = row + rank * (rows // 2)
    return jnp.where(slot >= rows, slot - rows, slot)


def allowed_keys(first_slot, start, rank, rows):
    n = first_slot.shape[0]
    key = slot_of(iota((n, rows), 1), rank, rows)
    query = slot_of(iota((n, 1), 0) + start, rank, rows)
    return (key <= query) & (key >= first_slot)


def attend_kernel(
    here_ref, own_ref, other_ref, gain_ref, wq_ref, bq_ref, wkv_ref, bkv_ref, wo_ref, place_ref,
    rope_ref, table_ref,
    first_t_ref, q_ref, k_ref, v_ref, att_ref, stat_ref, branch_ref, first_ref,
):
    rows = q_ref.shape[0]
    half = rows // 2
    heads = wq_ref.shape[0] // HEAD_SIZE
    scale = 0.5 / math.sqrt(HEAD_SIZE)
    highest = lax.Precision.HIGHEST
    wide = widen(heads)
    both_last = (((1,), (1,)), ((), ()))
    wq = dot(wide.astype(BF16), wq_ref[...]).astype(BF16)
    bq = lax.dot_general(
        bq_ref[...], wide, both_last, precision=highest, preferred_element_type=F32
    )
    wide_one = widen(1)
    wk = dot(wide_one.astype(BF16), wkv_ref[0]).astype(BF16)
    bk = lax.dot_general(
        bkv_ref[0:1], wide_one, both_last, precision=highest, preferred_element_type=F32
    )
    for r, src in enumerate((own_ref, other_ref)):
        part = pl.ds(r * half, half)
        x = src[...].astype(F32)
        inv = lax.rsqrt(jnp.mean(x * x, axis=1, keepdims=True) + EPS)
        first = (x * inv * gain_ref[...]).astype(BF16)
        first_ref[part, :] = first
        cosine, sine = wide_tables(rope_ref[part, :])
        q = nt(first, wq) + bq
        for h in range(heads):
            qh = q[:, h * WIDE : (h + 1) * WIDE]
            q_ref[part, h * WIDE : (h + 1) * WIDE] = (qh * cosine + rolled(qh) * sine).astype(BF16)
        k = nt(first, wk) + bk
        k_ref[part, :] = (k * cosine + rolled(k) * sine).astype(BF16)
        v = (nt(first, wkv_ref[1]) + bkv_ref[1:2]).astype(BF16)
        v_ref[part, :] = jnp.concatenate([v, jnp.zeros_like(v)], axis=1)
    first_t_ref[...] = permuted_rows(sent_rows(here_ref, table_ref, 2), first_ref[...])
    keys, v_even = k_ref[...], v_ref[...]
    v_odd = rolled(v_even.astype(F32)).astype(BF16)
    rank = here_ref[0]
    for r in range(2):
        part = pl.ds(r * half, half)
        ok = allowed_keys(place_ref[part, :], r * half, rank, rows)
        stat = jnp.zeros((half, WIDE), F32)
        lane = iota((half, WIDE), 1)
        pair = None
        for h in range(heads):
            s = nt(q_ref[part, h * WIDE : (h + 1) * WIDE], keys) * scale
            s = jnp.where(ok, s, -1e30)
            peak = jnp.max(s, axis=1, keepdims=True)
            e = jnp.exp(s - peak)
            total = jnp.sum(e, axis=1, keepdims=True)
            p = (e * (1.0 / total)).astype(BF16)
            stat = jnp.where(lane == h, peak + jnp.log(total), stat)
            a = dot(p, v_odd if h % 2 else v_even)
            if h % 2:
                att_ref[part, (h // 2) * WIDE : (h // 2 + 1) * WIDE] = (pair + a).astype(BF16)
            else:
                pair = a
        if heads % 2:
            att_ref[part, (heads - 1) * HEAD_SIZE :] = pair[:, :HEAD_SIZE].astype(BF16)
        stat_ref[part, :] = stat
        branch_ref[part, :] = dot(att_ref[part, :], wo_ref[...]).astype(BF16)


def attend(here, own, other, gain, wq, bq, wkv, bkv, wo, place, rope, table):
    rows, width = 2 * own.shape[0], own.shape[1]
    heads = wq.shape[0] // HEAD_SIZE
    sds = jax.ShapeDtypeStruct
    outs = (
        sds((width, rows), BF16),
        sds((rows, heads * WIDE), BF16),
        sds((rows, WIDE), BF16),
        sds((rows, WIDE), BF16),
        sds((rows, heads * HEAD_SIZE), BF16),
        sds((rows, WIDE), F32),
        sds((rows, width), BF16),
    )
    return pl.pallas_call(
        attend_kernel,
        out_shape=outs,
        in_specs=[pl.BlockSpec(memory_space=pltpu.SMEM)]
        + [pl.BlockSpec(memory_space=pltpu.VMEM)] * 11,
        out_specs=[pl.BlockSpec(memory_space=pltpu.VMEM)] * 7,
        scratch_shapes=[pltpu.VMEM((rows, width), BF16)],
        compiler_params=pltpu.CompilerParams(vmem_limit_bytes=VMEM_LIMIT),
        cost_estimate=pl.CostEstimate(flops=5_000_000_000, bytes_accessed=8_000_000, transcendentals=0),
        name="attention_forward",
    )(here, own, other, gain, wq, bq, wkv, bkv, wo, place, rope, table)


def feed_forward_kernel(
    own_ref, other_ref, branch_ref, far_ref, gain_ref, og_own_ref, og_other_ref, wgu_ref, wd_ref,
    down_ref, dg_ref, du_ref, mid_ref, second_ref, res_ref, send_ref, ds_ref, gainsum_ref,
    og_ref, ot_ref, mlp_ref, acc_ref,
):
    step = pl.program_id(0)
    last = pl.num_programs(0) - 1
    half, width = own_ref.shape

    @pl.when(step == 0)
    def _():
        for r, tok in enumerate((own_ref, other_ref)):
            a, b = pl.ds(r * half, half), pl.ds((1 - r) * half, half)
            mid = tok[...].astype(F32) + (
                branch_ref[a, :].astype(F32) + far_ref[b, :].astype(F32)
            )
            mid_ref[a, :] = mid
            inv = lax.rsqrt(jnp.mean(mid * mid, axis=1, keepdims=True) + EPS)
            second_ref[a, :] = (mid * inv * gain_ref[...]).astype(BF16)
        for r, og in enumerate((og_own_ref, og_other_ref)):
            og_ref[r * half : (r + 1) * half, :] = og[...]
            ot_ref[:, r * half : (r + 1) * half] = og[...].T
        mlp_ref[...] = jnp.zeros_like(mlp_ref)
        acc_ref[...] = jnp.zeros_like(acc_ref)

    def units(n):
        wg, wu, wd = wgu_ref[0, :, :n], wgu_ref[1, :, :n], wd_ref[:n, :]
        second = second_ref[...]
        gate, up = dot(second, wg), dot(second, wu)
        d_hidden = nt(og_ref[...], wd)
        sigmoid = 1.0 / (1.0 + jnp.exp(-gate))
        act = gate * sigmoid
        hidden = (act * up).astype(BF16)
        d_gate = (d_hidden * up * (sigmoid * (1.0 + gate * (1.0 - sigmoid)))).astype(BF16)
        d_up = (d_hidden * act).astype(BF16)
        dg_ref[:, :n] = d_gate
        du_ref[:, :n] = d_up
        down_ref[:, :n] = dot(ot_ref[...], hidden).astype(BF16)
        mlp_ref[...] += dot(hidden, wd)
        acc_ref[...] += nt(d_gate, wg) + nt(d_up, wu)

    full = wd_ref.shape[0]
    tail = FF_LOCAL % full

    @pl.when(step < last)
    def _():
        units(full)

    @pl.when(step == last)
    def _():
        units(tail or full)
        res_ref[...] = mid_ref[:half, :] + mlp_ref[:half, :]
        send_ref[...] = mlp_ref[half:, :].astype(BF16)
        ds = acc_ref[...]
        ds_ref[...] = ds.astype(BF16)
        mid = mid_ref[...]
        normed = mid * lax.rsqrt(jnp.mean(mid * mid, axis=1, keepdims=True) + EPS)
        gainsum_ref[...] = jnp.sum(ds * normed, axis=0, keepdims=True)


def unit_products_kernel(
    here_ref, second_ref, table_ref, dg_ref, du_ref,
    g0_ref, g1_ref, g2_ref, g3_ref, u0_ref, u1_ref, u2_ref, u3_ref,
    gt_ref, ut_ref,
):
    quarter = g0_ref.shape[0]

    @pl.when(pl.program_id(0) == 0)
    def _():
        gt_ref[...] = permuted_rows(sent_rows(here_ref, table_ref, 0), second_ref[...])
        ut_ref[...] = permuted_rows(sent_rows(here_ref, table_ref, 1), second_ref[...])

    for k, ref in enumerate((g0_ref, g1_ref, g2_ref, g3_ref)):
        ref[...] = dot(gt_ref[k * quarter : (k + 1) * quarter, :], dg_ref[...]).astype(BF16)
    for k, ref in enumerate((u0_ref, u1_ref, u2_ref, u3_ref)):
        ref[...] = dot(ut_ref[k * quarter : (k + 1) * quarter, :], du_ref[...]).astype(BF16)


FF_LOCAL = 2432
FF_BLOCK = 512


def feed_forward(own, other, branch, far, gain, og_own, og_other, wgu, wd):
    half, width = own.shape
    rows = 2 * half
    ff = wd.shape[0]
    sds = jax.ShapeDtypeStruct
    units = pl.BlockSpec((rows, FF_BLOCK), lambda i: (0, i))
    return pl.pallas_call(
        feed_forward_kernel,
        grid=(-(-ff // FF_BLOCK),),
        out_shape=[
            sds((width, ff), BF16),
            sds((rows, ff), BF16),
            sds((rows, ff), BF16),
            sds((rows, width), F32),
            sds((rows, width), BF16),
            sds((half, width), F32),
            sds((half, width), BF16),
            sds((rows, width), BF16),
            sds((1, width), F32),
        ],
        in_specs=[
            whole(half, width), whole(half, width), whole(rows, width), whole(rows, width),
            whole(1, width), whole(half, width), whole(half, width),
            pl.BlockSpec((2, width, FF_BLOCK), lambda i: (0, 0, i)),
            pl.BlockSpec((FF_BLOCK, width), lambda i: (i, 0)),
        ],
        out_specs=[
            pl.BlockSpec((width, FF_BLOCK), lambda i: (0, i)), units, units,
            whole(rows, width), whole(rows, width), whole(half, width), whole(half, width),
            whole(rows, width), whole(1, width),
        ],
        scratch_shapes=[
            pltpu.VMEM((rows, width), BF16),
            pltpu.VMEM((width, rows), BF16),
            pltpu.VMEM((rows, width), F32),
            pltpu.VMEM((rows, width), F32),
        ],
        compiler_params=pltpu.CompilerParams(vmem_limit_bytes=VMEM_LIMIT),
        cost_estimate=pl.CostEstimate(flops=18_000_000_000, bytes_accessed=40_000_000, transcendentals=0),
        name="feed_forward",
    )(own, other, branch, far, gain, og_own, og_other, wgu, wd)


def unit_products(here, second, table, d_gate, d_up):
    rows, width = second.shape
    ff = d_gate.shape[1]
    q = width // RING
    piece = pl.BlockSpec((q, FF_BLOCK), lambda i: (0, i))
    units = pl.BlockSpec((rows, FF_BLOCK), lambda i: (0, i))
    return pl.pallas_call(
        unit_products_kernel,
        grid=(-(-ff // FF_BLOCK),),
        out_shape=[jax.ShapeDtypeStruct((q, ff), BF16)] * 8,
        in_specs=[
            pl.BlockSpec(memory_space=pltpu.SMEM), whole(rows, width), whole(*table.shape),
            units, units,
        ],
        out_specs=[piece] * 8,
        scratch_shapes=[pltpu.VMEM((width, rows), BF16)] * 2,
        compiler_params=pltpu.CompilerParams(vmem_limit_bytes=VMEM_LIMIT),
        cost_estimate=pl.CostEstimate(flops=7_000_000_000, bytes_accessed=16_000_000, transcendentals=0),
        name="unit_products",
    )(here, second, table, d_gate, d_up)


def attend_back_kernel(
    here_ref, mid_ref, ds_ref, far_ref, og_own_ref, og_other_ref, gain_ref, att_ref, table_ref,
    wo_ref, q_ref, k_ref, v_ref, stat_ref, place_ref, rope_ref,
    wq_ref, wkv_ref, first_t_ref, own_ref, other_ref,
    block_ref, d_mid_ref, d_own_ref, d_send_ref, gainsum_ref, bias_ref,
    d_branch_ref, d_all_ref, dk_ref, dv_ref,
):
    rows = q_ref.shape[0]
    half = rows // 2
    for r, og in enumerate((og_own_ref, og_other_ref)):
        a, b = pl.ds(r * half, half), pl.ds((1 - r) * half, half)
        mid = mid_ref[a, :]
        inv = lax.rsqrt(jnp.mean(mid * mid, axis=1, keepdims=True) + EPS)
        normed = mid * inv
        d = (ds_ref[a, :].astype(F32) + far_ref[b, :].astype(F32)) * gain_ref[...]
        d_mid = og[...].astype(F32) + inv * (
            d - normed * jnp.mean(d * normed, axis=1, keepdims=True)
        )
        if r == 0:
            d_mid_ref[...] = d_mid
        d_branch_ref[a, :] = d_mid.astype(BF16)
    heads = wq_ref.shape[0] // HEAD_SIZE
    scale = 0.5 / math.sqrt(HEAD_SIZE)
    rank = here_ref[0]
    keys, v_even = k_ref[...], v_ref[...]
    v_odd = rolled(v_even.astype(F32)).astype(BF16)
    low = iota((half, WIDE), 1) < HEAD_SIZE
    low_all = iota((rows, WIDE), 1) < HEAD_SIZE
    dk_ref[...] = jnp.zeros_like(dk_ref)
    dv_ref[...] = jnp.zeros_like(dv_ref)

    def back(x, cosine, sine):
        return x * cosine - rolled(x) * sine

    for r in range(2):
        part = pl.ds(r * half, half)
        ok = allowed_keys(place_ref[part, :], r * half, rank, rows)
        cosine, sine = wide_tables(rope_ref[part, :])
        d_att = nt(d_branch_ref[part, :], wo_ref[...]).astype(BF16)
        pair = None
        for h in range(heads):
            tile = h // 2
            qh = q_ref[part, h * WIDE : (h + 1) * WIDE]
            da = d_att[:, tile * WIDE : (tile + 1) * WIDE]
            if da.shape[1] < WIDE:
                da = jnp.concatenate([da, jnp.zeros_like(da)], axis=1)
            s = nt(qh, keys) * scale
            p = jnp.where(ok, jnp.exp(s - stat_ref[part, h : h + 1]), 0.0)
            dp = nt(da, v_odd if h % 2 else v_even)
            ds = (p * (dp - jnp.sum(p * dp, axis=1, keepdims=True))).astype(BF16)
            pb = p.astype(BF16)
            dk_ref[...] += tn(ds, qh)
            dv = tn(pb, da)
            dv_ref[...] += jnp.where(low_all if h % 2 == 0 else ~low_all, dv, 0.0)
            dq = back(dot(ds, keys) * (2.0 * scale), cosine, sine)
            if h % 2:
                d_all_ref[part, tile * WIDE : (tile + 1) * WIDE] = jnp.where(
                    low, pair, rolled(dq)
                ).astype(BF16)
            else:
                pair = dq
        if heads % 2:
            d_all_ref[part, (heads - 1) * HEAD_SIZE : heads * HEAD_SIZE] = pair[
                :, :HEAD_SIZE
            ].astype(BF16)
    n = heads * HEAD_SIZE
    dk = back(dk_ref[...] * (2.0 * scale), *wide_tables(rope_ref[...]))[:, :HEAD_SIZE].astype(BF16)
    dv = dv_ref[...]
    dv = (dv + rolled(dv))[:, :HEAD_SIZE].astype(BF16)
    d_all_ref[:, n : n + HEAD_SIZE] = dk
    d_all_ref[:, n + HEAD_SIZE :] = dv
    d_all = d_all_ref[...]
    m = n + 2 * HEAD_SIZE
    block_ref[:, :m] = dot(first_t_ref[...], d_all).astype(BF16)
    left = permuted_rows(sent_rows(here_ref, table_ref, 2), d_branch_ref[...])
    block_ref[:, m:] = dot(left, att_ref[...]).astype(BF16)
    bias_ref[...] = jnp.sum(d_all.astype(F32), axis=0, keepdims=True)
    total = jnp.zeros((1, own_ref.shape[1]), F32)
    for r, src in enumerate((own_ref, other_ref)):
        part = pl.ds(r * half, half)
        d_first = (
            dot(d_all_ref[part, :n], wq_ref[...])
            + dot(d_all_ref[part, n : n + HEAD_SIZE], wkv_ref[0])
            + dot(d_all_ref[part, n + HEAD_SIZE :], wkv_ref[1])
        )
        x = src[...].astype(F32)
        normed = x * lax.rsqrt(jnp.mean(x * x, axis=1, keepdims=True) + EPS)
        total = total + jnp.sum(d_first * normed, axis=0, keepdims=True)
        if r == 0:
            d_own_ref[...] = d_first
        else:
            d_send_ref[...] = d_first.astype(BF16)
    gainsum_ref[...] = total


def attend_back(
    here, mid, ds, far, og_own, og_other, gain, att, table,
    wo, q, k, v, stat, place, rope, wq, wkv, first_t, own, other,
):
    rows, width = mid.shape
    n = wq.shape[0] + 2 * HEAD_SIZE
    sds = jax.ShapeDtypeStruct
    return pl.pallas_call(
        attend_back_kernel,
        out_shape=(
            sds((width, n + att.shape[1]), BF16),
            sds((rows // 2, width), F32),
            sds((rows // 2, width), F32),
            sds((rows // 2, width), BF16),
            sds((1, width), F32),
            sds((1, n), F32),
        ),
        in_specs=[pl.BlockSpec(memory_space=pltpu.SMEM)]
        + [pl.BlockSpec(memory_space=pltpu.VMEM)] * 20,
        out_specs=[pl.BlockSpec(memory_space=pltpu.VMEM)] * 6,
        scratch_shapes=[
            pltpu.VMEM((rows, width), BF16),
            pltpu.VMEM((rows, n), BF16),
            pltpu.VMEM((rows, WIDE), F32),
            pltpu.VMEM((rows, WIDE), F32),
        ],
        compiler_params=pltpu.CompilerParams(vmem_limit_bytes=VMEM_LIMIT),
        cost_estimate=pl.CostEstimate(flops=12_000_000_000, bytes_accessed=16_000_000, transcendentals=0),
        name="attention_backward",
    )(
        here, mid, ds, far, og_own, og_other, gain, att, table,
        wo, q, k, v, stat, place, rope, wq, wkv, first_t, own, other,
    )


def high_low(x):
    high = x.astype(BF16)
    return high, (x - high.astype(F32)).astype(BF16)


def put_sums(ref, row, sums):
    high, low = high_low(sums)
    ref[row : row + SUM_ROWS, :SUM_LANES] = high
    ref[row : row + SUM_ROWS, SUM_LANES : 2 * SUM_LANES] = low


def get_sums(ref, row):
    high = ref[row : row + SUM_ROWS, :SUM_LANES].astype(F32)
    return high + ref[row : row + SUM_ROWS, SUM_LANES : 2 * SUM_LANES].astype(F32)


def up_to(n, m):
    return -(-n // m) * m


def local_call(kernel, name, out_shape, *args, carried=None):
    vmem = pl.BlockSpec(memory_space=pltpu.VMEM)
    n, m = len(args), len(out_shape)
    extra = [] if carried is None else [carried]

    def kernel_alone(*refs):
        kernel(*refs[:n], *refs[n + len(extra) : n + len(extra) + m])

    return pl.pallas_call(
        kernel_alone,
        out_shape=[jax.ShapeDtypeStruct(shape, dtype) for shape, dtype in out_shape]
        + [jax.ShapeDtypeStruct(x.shape, x.dtype) for x in extra],
        in_specs=[vmem] * n + [pl.BlockSpec(memory_space=pl.ANY)] * len(extra),
        out_specs=[vmem] * m + [pl.BlockSpec(memory_space=pl.ANY)] * len(extra),
        input_output_aliases={n: m} if extra else {},
        compiler_params=pltpu.CompilerParams(vmem_limit_bytes=VMEM_LIMIT),
        cost_estimate=pl.CostEstimate(flops=1_000_000_000, bytes_accessed=8_000_000, transcendentals=0),
        name=name,
    )(*args, *extra)


def first_sums_kernel(
    gl_ref, gr_ref, g2_ref, ul_ref, ur_ref, u2_ref, a_ref, gains_ref, bias_ref,
    yr_ref, yl_ref, y2_ref, xr_ref, xl_ref, sums_ref,
):
    h = g2_ref.shape[0] // 2
    ff = g2_ref.shape[1]
    width = gains_ref.shape[1]
    sums_ref[...] = jnp.zeros_like(sums_ref)
    rest = width - SUM_LANES
    for k in range(2):
        sums_ref[2 * k : 2 * k + 1, :] = gains_ref[k : k + 1, :SUM_LANES]
        sums_ref[2 * k + 1 : 2 * k + 2, :rest] = gains_ref[k : k + 1, SUM_LANES:]
    rest = bias_ref.shape[1] - SUM_LANES
    sums_ref[4:5, :] = bias_ref[:, :SUM_LANES]
    sums_ref[5:6, :rest] = bias_ref[:, SUM_LANES:]
    sums = sums_ref[...]
    for k, (ref, low, heard) in enumerate(((yr_ref, 0, gl_ref), (yl_ref, h, gr_ref))):
        later = g2_ref[low : low + h, :].astype(F32)
        ref[:h, :ff] = (later + heard[:h, :].astype(F32)).astype(BF16)
        n = a_ref.shape[1]
        ref[:h, ff : ff + n] = a_ref[2 * k * h : (2 * k + 1) * h, :]
        ref[:h, ff + n :] = a_ref[(2 * k + 1) * h : (2 * k + 2) * h, :]
        put_sums(ref, h, sums)
    for k, (ref, low, heard) in enumerate(((xr_ref, 0, ul_ref), (xl_ref, h, ur_ref))):
        later = u2_ref[low : low + h, :].astype(F32)
        ref[...] = (later + heard[:h, :].astype(F32)).astype(BF16)
    y2_ref[: 2 * h, :] = a_ref[4 * h : 6 * h, :]
    put_sums(y2_ref, 2 * h, sums)
    high, low = high_low(sums)
    sums_ref[...] = high.astype(F32) + low.astype(F32)


def first_sums(gate_first, g2, up_first, u2, a, gains, bias):
    h, ff = g2.shape[0] // 2, g2.shape[1]
    n = a.shape[1]
    y, x = (h + SUM_ROWS, ff + 2 * n), (h, ff)
    outs = [
        (y, BF16), (y, BF16), ((2 * h + SUM_ROWS, n), BF16),
        (x, BF16), (x, BF16), ((SUM_ROWS, SUM_LANES), F32),
    ]
    return local_call(
        first_sums_kernel, "first_sums", outs, *gate_first, g2, *up_first, u2, a, gains, bias
    )


def second_sums_kernel(
    yl_ref, yr_ref, y2_ref, xl_ref, xr_ref,
    gl_ref, gr_ref, g3_ref, ul_ref, ur_ref, u3_ref, mine_ref, sums_ref,
    p0_ref, p1_ref, p2_ref, own_a_ref, q0_ref, q1_ref, q2_ref, own_b_ref, out_sums_ref,
):
    h = g3_ref.shape[0] // 2
    q = h // 2
    ff = g3_ref.shape[1]
    n = mine_ref.shape[1]
    sums = (sums_ref[...] + get_sums(y2_ref, 2 * h)) + (get_sums(yl_ref, h) + get_sums(yr_ref, h))
    high, low = high_low(sums)
    out_sums_ref[...] = high.astype(F32) + low.astype(F32)
    groups = (
        ((p0_ref, p1_ref, p2_ref, own_a_ref), (gr_ref, yl_ref), (gl_ref, yr_ref), g3_ref),
        ((q0_ref, q1_ref, q2_ref, own_b_ref), (ur_ref, xl_ref), (ul_ref, xr_ref), u3_ref),
    )
    for refs, *heard, kept in groups:
        for k, (first, second) in enumerate(heard):
            big = (
                kept[k * h : (k + 1) * h, :].astype(F32)
                + first[h:, :].astype(F32)
                + second[:h, :ff].astype(F32)
            )
            for j in range(2):
                ref = refs[2 * k + j]
                ref[:q, :ff] = big[j * q : (j + 1) * q, :].astype(ref.dtype)
    for k in range(2):
        at = slice(ff + k * n, ff + (k + 1) * n)
        part = slice(k * h, (k + 1) * h)
        small = (
            mine_ref[6 * h + k * h : 6 * h + (k + 1) * h, :].astype(F32)
            + y2_ref[part, :].astype(F32)
            + (yl_ref[:h, at].astype(F32) + yr_ref[:h, at].astype(F32))
        )
        for j in range(2):
            ref = (p0_ref, p1_ref, p2_ref, own_a_ref)[2 * k + j]
            ref[:q, ff:] = small[j * q : (j + 1) * q, :].astype(ref.dtype)
    for ref in (p0_ref, p1_ref, p2_ref):
        put_sums(ref, q, sums)


def second_sums(y_heard, x_heard, gate_first, g3, up_first, u3, mine, sums, carried):
    h, ff = g3.shape[0] // 2, g3.shape[1]
    q, n = h // 2, ff + mine.shape[1]
    outs = (
        [((q + SUM_ROWS, n), BF16)] * 3 + [((q, n), F32)]
        + [((q, ff), BF16)] * 3 + [((q, ff), F32)]
        + [((SUM_ROWS, SUM_LANES), F32)]
    )
    return local_call(
        second_sums_kernel, "second_sums", outs,
        *y_heard, *x_heard, *gate_first, g3, *up_first, u3, mine, sums, carried=carried,
    )


def third_sums_kernel(
    p0_ref, p1_ref, p2_ref, own_a_ref, q0_ref, q1_ref, q2_ref, own_b_ref, sums_ref,
    r0_ref, r1_ref, r2_ref, own_ref, out_sums_ref,
):
    q, wa = own_a_ref.shape
    r = q // RING
    sums = (sums_ref[...] + get_sums(p2_ref, q)) + (get_sums(p0_ref, q) + get_sums(p1_ref, q))
    high, low = high_low(sums)
    out_sums_ref[...] = high.astype(F32) + low.astype(F32)
    a = own_a_ref[...] + (
        p0_ref[:q, :].astype(F32) + p1_ref[:q, :].astype(F32) + p2_ref[:q, :].astype(F32)
    )
    b = own_b_ref[...] + (
        q0_ref[...].astype(F32) + q1_ref[...].astype(F32) + q2_ref[...].astype(F32)
    )
    for k, ref in enumerate((r0_ref, r1_ref, r2_ref)):
        put_sums(ref, 0, sums)
        ref[SUM_ROWS : SUM_ROWS + r, :wa] = a[k * r : (k + 1) * r, :].astype(BF16)
        ref[SUM_ROWS : SUM_ROWS + r, wa:] = b[k * r : (k + 1) * r, :].astype(BF16)
    own_ref[:r, :wa] = a[3 * r :, :]
    own_ref[:r, wa:] = b[3 * r :, :]


def third_sums(heard_a, own_a, heard_b, own_b, sums, carried):
    r = own_a.shape[0] // RING
    n = own_a.shape[1] + own_b.shape[1]
    rows = up_to(SUM_ROWS + r, SUM_ROWS)
    outs = [((rows, n), BF16)] * 3 + [
        ((up_to(r, SUM_ROWS), n), F32), ((SUM_ROWS, SUM_LANES), F32)
    ]
    return local_call(
        third_sums_kernel, "third_sums", outs, *heard_a, own_a, *heard_b, own_b, sums,
        carried=carried,
    )


def last_sums_kernel(
    r0_ref, r1_ref, r2_ref, own_ref, sums_ref,
    gate_up_ref, query_ref, pair_ref, out_ref, gains_ref, query_bias_ref, pair_bias_ref,
):
    r, ff = gate_up_ref.shape[0], gate_up_ref.shape[2]
    n = query_ref.shape[1]
    sums = (sums_ref[...] + get_sums(r2_ref, 0)) + (get_sums(r0_ref, 0) + get_sums(r1_ref, 0))
    rest = gains_ref.shape[1] - SUM_LANES
    for k in range(2):
        gains_ref[k : k + 1, :SUM_LANES] = sums[2 * k : 2 * k + 1, :]
        gains_ref[k : k + 1, SUM_LANES:] = sums[2 * k + 1 : 2 * k + 2, :rest]
    query_bias_ref[...] = sums[4:5, :n]
    pair_bias_ref[0:1, :] = sums[4:5, n : n + HEAD_SIZE]
    pair_bias_ref[1:2, :] = sums[5:6, :HEAD_SIZE]
    part = slice(SUM_ROWS, SUM_ROWS + r)
    total = own_ref[:r, :] + (
        r0_ref[part, :].astype(F32) + r1_ref[part, :].astype(F32) + r2_ref[part, :].astype(F32)
    )
    m = ff + n + 2 * HEAD_SIZE
    gate_up_ref[:, 0, :] = total[:, :ff]
    gate_up_ref[:, 1, :] = total[:, m + n :]
    query_ref[...] = total[:, ff : ff + n]
    pair_ref[:, 0, :] = total[:, ff + n : ff + n + HEAD_SIZE]
    pair_ref[:, 1, :] = total[:, ff + n + HEAD_SIZE : ff + n + 2 * HEAD_SIZE]
    out_ref[...] = total[:, m : m + n]


def last_sums(heard, own, sums, ff, n, r, width):
    outs = [
        ((r, 2, ff), F32), ((r, n), F32), ((r, 2, HEAD_SIZE), F32), ((r, n), F32),
        ((2, width), F32), ((1, n), F32), ((2, HEAD_SIZE), F32),
    ]
    return local_call(last_sums_kernel, "last_sums", outs, *heard, own, sums)


def body(
    tokens,
    out_grad,
    first_gain,
    query_weight,
    query_bias,
    key_value_weight_pair,
    key_value_bias_pair,
    output_weight,
    second_gain,
    gate_up_weight,
    down_weight,
    lengths,
    group_of,
):
    own_rows, width = tokens.shape
    rows = 2 * own_rows
    tensor_rank = lax.axis_index("tensor")
    data_group = lax.axis_index(DP)
    heads = query_weight.shape[1] // HEAD_SIZE
    per_device = width // 64
    tokens_other = swap(tokens)
    og_other = swap(out_grad)
    query_weight_t = query_weight.T
    pair_weight_t = jnp.swapaxes(key_value_weight_pair, 1, 2)
    slots = jnp.arange(rows, dtype=jnp.int32) + tensor_rank * own_rows
    slots = jnp.where(slots >= rows, slots - rows, slots)
    first_slot = layout(lengths, group_of, data_group, slots)
    rope = rope_table(slots - first_slot)
    place = first_slot[:, None]
    here = jnp.stack([tensor_rank, *[lax.axis_index(axis) for axis in DP]])
    table = jnp.asarray(offset_table(per_device))
    gain1, gain2 = first_gain[None, :], second_gain[None, :]
    first_t, q, k, v, attended, stat, branch = attend(
        here, tokens, tokens_other, gain1, query_weight_t, query_bias[None, :],
        pair_weight_t, key_value_bias_pair, output_weight, place, rope, table,
    )
    branch, og_other = pinned(branch, og_other)
    down, d_gate, d_up, middle, second, res, mlp_send, ds, gain2_part = feed_forward(
        tokens, tokens_other, branch, swap(branch), gain2, out_grad, og_other,
        gate_up_weight, down_weight,
    )
    ds_far = swap(ds)
    g0, g1, g2, g3, u0, u1, u2, u3 = unit_products(here, second, table, d_gate, d_up)
    down, g0, g1, u0, u1 = pinned(down, g0, g1, u0, u1)
    down = scatter_natural(down, DP[0])
    z_axis, y_axis, x_axis = DP
    gate_first = ring_first(g0, g1, y_axis)
    up_first = ring_first(u0, u1, x_axis)
    result = (res + swap(mlp_send).astype(F32)).astype(BF16)
    block, d_middle, d_own, d_send, gain1_part, bias_part = attend_back(
        here, middle, ds, ds_far, out_grad, og_other, gain2, attended, table,
        output_weight, q, k, v, stat, place, rope,
        query_weight_t, pair_weight_t, first_t, tokens, tokens_other,
    )
    gains = jnp.concatenate([gain1_part, gain2_part], axis=0)
    gains = gains + swap(gains)
    yr, yl, y2, xr, xl, sums = first_sums(
        gate_first, g2, up_first, u2, block, gains, bias_part
    )
    y_heard = to_others((yr, yl, y2), y_axis)
    x_heard = ring_first(xr, xl, x_axis)
    p0, p1, p2, own_a, q0, q1, q2, own_b, sums, down = second_sums(
        y_heard, x_heard, gate_first, g3, up_first, u3, block, sums, down
    )
    down = scatter_natural(down, DP[1])
    heard_a = to_others((p0, p1, p2), x_axis)
    heard_b = to_others((q0, q1, q2), y_axis)
    r0, r1, r2, own, sums, down = third_sums(heard_a, own_a, heard_b, own_b, sums, down)
    down = scatter_natural(down, DP[2])
    heard = to_others((r0, r1, r2), z_axis)
    n = heads * HEAD_SIZE
    ff = down.shape[1]
    gate_up, grad_query, grad_pair, grad_output, gains, query_bias, pair_bias = last_sums(
        heard, own, sums, ff, n, per_device, width
    )

    inputs = tokens.astype(F32)
    inv_first = lax.rsqrt(jnp.mean(inputs * inputs, axis=1, keepdims=True) + EPS)
    own_normed = inputs * inv_first
    d_normed = (d_own + swap(d_send).astype(F32)) * first_gain
    grad_tokens = d_middle + inv_first * (
        d_normed - own_normed * jnp.mean(d_normed * own_normed, axis=1, keepdims=True)
    )
    return (
        result,
        grad_tokens,
        gains[0],
        grad_query,
        query_bias[0],
        jnp.swapaxes(grad_pair, 0, 1),
        pair_bias,
        grad_output.T,
        gains[1],
        jnp.swapaxes(gate_up, 0, 1),
        down.astype(F32).T,
    )


def solution(mesh):
    torus = Mesh(
        mesh.devices.reshape(4, 4, 4, mesh.shape["tensor"]), ("dp_0", "dp_1", "dp_2", "tensor")
    )
    placed = (
        P(DP_TENSOR, None),
        P(DP_TENSOR, None),
        P(),
        P(None, "tensor"),
        P("tensor"),
        P(None, None, "tensor"),
        P(None, "tensor"),
        P("tensor", None),
        P(),
        P(None, None, "tensor"),
        P("tensor", None),
        P(),
        P(),
    )
    return jax.shard_map(
        body,
        mesh=torus,
        in_specs=placed,
        out_specs=(
            P(DP_TENSOR, None),
            P(DP_TENSOR, None),
            P(),
            P(DP, "tensor"),
            P("tensor"),
            P(None, DP, "tensor"),
            P(None, "tensor"),
            P("tensor", DP),
            P(),
            P(None, DP, "tensor"),
            P("tensor", DP),
        ),
        check_vma=False,
    )
```
